512 devices in a mesh: box: 64 (over y, z_lo, core), samp: 8 (over x, z_hi).
Axes of the slice: x: 4, y: 4, z: 16 (z_hi: 2, z_lo: 8; z = z_hi * 8 + z_lo), core: 2. Of those that a mesh axis runs over, the one named last changes fastest.
Arguments:
- currents: bfloat16 [16, 2, 32768], P(None, None, 'box'), may hold values from -6 to 6
- radiation: bfloat16 [2, 512, 64, 2048], P(None, 'box', None, 'samp'), may hold values from -0.5 to 0.5
- interp: bfloat16 [2, 3, 2, 2048, 256], P(None, None, None, 'samp'), may hold values from -0.1875 to 0.1875
- translation: bfloat16 [2, 316, 2048], P(None, None, 'samp'), may hold values from -1 to 1
- inter_owner: int32 [512, 4], P('box'), may hold values from 0 to 63, all different within a row; in each aligned block of 8 rows (0 to 7, 8 to 15, ...) at most 2 rows name the same one
- inter_local: int32 [512, 4, 2], P('box'), may hold values from 0 to 7
- inter_type: int32 [512, 4, 2], P('box'), may hold values from 0 to 315
- near_blocks: bfloat16 [2, 16384, 64, 64], P(None, ('box', 'samp')), may hold values from -0.09375 to 0.09375
- near_index: int32 [16384, 2], P(('box', 'samp')), may hold values from 0 to 511, as said below
Outputs:
- field: float32 [16, 2, 32768], P('samp', None, 'box')
The draws below stay inside these ranges and needn't reach their ends.
Inputs may be any that keep to these rules, and one draw needn't show every extreme that they name: `inter_owner`: each box names 4 different owners; among the 8 boxes of one box index no owner is named more than 2 times. `near_index`: the blocks of one device receive on boxes of that device's box index; each source box is one of those boxes or of the 8 boxes on either side.
All inputs are finite; a program needn't handle non-finite values.
Results may differ from the reference program's by a relative error of at most 0.0075.
Values may be sent and summed in bfloat16 or wider, within the bound.
A program may use at most 64 MiB of HBM per device.

```python
import math
import jax
import jax.numpy as jnp
import numpy as np
from jax import lax

M = 64
K = 2048
TYPES = 316
R = 16
BOX_DEV = 8
NEAR_DEV = 32
OWN = 4
PER = 2
SAMP_DEV = 256
LEVELS = 3
BOXES = 512
CAP = 2
NEAR = 16384
N_BOX = 64
N_SAMP = 8


def draw_near_index(key, part):
    key = jax.random.fold_in(key, 11)
    key_target, key_source, key_backup = jax.random.split(key, 3)
    position = jnp.arange(NEAR, dtype=jnp.int32)
    group_first = position // NEAR_DEV // N_SAMP * BOX_DEV
    target = group_first + jax.random.randint(key_target, (NEAR,), 0, BOX_DEV, dtype=jnp.int32)
    candidate = group_first + jax.random.randint(key_source, (NEAR,), -BOX_DEV, 2 * BOX_DEV, dtype=jnp.int32)
    backup = group_first + jax.random.randint(key_backup, (NEAR,), 0, BOX_DEV, dtype=jnp.int32)
    inside = (candidate >= 0) & (candidate < BOXES)
    source = jnp.where(inside, candidate, backup)
    return jnp.stack([target, source], axis=1).astype(jnp.int32)


def touch_ends(drawn, rng, low, high):
    index_at = [jax.random.randint(jax.random.fold_in(rng, axis), (), 0, length) for axis, length in enumerate(drawn.shape)]
    main_axis = drawn.shape.index(max(drawn.shape))
    beside = index_at[:main_axis] + [(index_at[main_axis] + 1) % drawn.shape[main_axis]] + index_at[main_axis + 1:]
    return drawn.at[tuple(index_at)].set(low).at[tuple(beside)].set(high)


def shard_levels(key, dims, pieces, least, high):
    loudness = 1.0
    for dim, parts in pieces:
        heights = jax.random.uniform(jax.random.fold_in(jax.random.fold_in(key, 6), dim), (parts,), jnp.float32, least / len(pieces), high / len(pieces))
        loudness = loudness * jnp.repeat(jnp.exp(heights), dims[dim] // parts).reshape((-1,) + (1,) * (len(dims) - 1 - dim))
    return loudness


def deal_out(own_key, own, number, rows, number_of, top, most, lean):
    sequence = jax.random.permutation(own_key, number_of)
    crowded, common = portions_of(number_of, rows * top, most, lean, True), portions_of(number_of, rows * top, most, lean, False)
    places = jnp.arange(number_of)

    def named(lengths, offset_by):
        used = int((lengths > 0).sum())
        fixed = max(1, used // 4)
        passed = fixed + (places - fixed + offset_by * (used - fixed)) % max(1, number_of - fixed)
        return jnp.zeros((number_of,), jnp.int32).at[sequence[jnp.where(places < fixed, places, passed)]].set(jnp.asarray(lengths, jnp.int32))

    lengths = jnp.where(number % 4 == 0, named(crowded, number // 4), named(common, number - number // 4 - 1))
    mixed = jax.random.permutation(jax.random.fold_in(own, 3), number_of)
    source_of, sink = mixed[0:number_of // 2 * 2:2], mixed[1:number_of // 2 * 2:2]
    margin = jnp.minimum(lengths[source_of] - 1, most - lengths[sink]) // 2
    margin = jnp.where((source_of == sequence[0]) | (sink == sequence[0]) | (lengths[sink] == 0), 0, jnp.maximum(margin, 0))
    passed = jax.random.randint(jax.random.fold_in(own, 4), (number_of // 2,), 0, 1 << 20) % (margin + 1)
    lengths = lengths.at[source_of].add(-passed).at[sink].add(passed)
    labels = jnp.searchsorted(jnp.cumsum(lengths), jnp.arange(rows * top), side="right").astype(jnp.int32)
    listing = labels.reshape(top, rows).T
    listing = listing[jax.random.permutation(jax.random.fold_in(own, 1), rows)]
    offset_by = jax.random.randint(jax.random.fold_in(own, 2), (rows, 1), 0, top)
    return jnp.take_along_axis(listing, (jnp.arange(top)[None, :] + offset_by) % top, axis=1)


def portions_of(number_of, total, limit, skew, full):
    portions = [(1 << 20) // math.isqrt(grade ** skew) + 1 for grade in range(1, number_of + 1)]
    largest = limit if full else min(limit, max(-(-total // number_of), total * portions[0] // sum(portions)))
    least = 1 if total - largest >= number_of - 1 else 0
    given, spare = [largest] + [least] * (number_of - 1), total - largest - least * (number_of - 1)
    while spare > 0:
        candidates = [i for i in range(1, number_of) if given[i] < largest] or [i for i in range(1, number_of) if given[i] < limit]
        pool, budget = sum([portions[i] for i in candidates]), spare
        for i in candidates:
            extra = min(limit - given[i], max(1, budget * portions[i] // pool), spare)
            given[i] = given[i] + extra
            spare = spare - extra
    return np.array(given)


def normal_values(stream_key, shape, scale, limit, pieces=(), held_as=jnp.bfloat16):
    values = jax.random.normal(stream_key, shape, jnp.float32) * scale
    if len(pieces) > 0:
        values = shard_levels(stream_key, shape, pieces, -0.22, 0.18) * values
    return jnp.clip(values, min=-limit, max=limit).astype(held_as)


def setup_inputs(seed: int = 0) -> dict:
    keys = jax.random.split(jax.random.key(seed), 10)
    currents = normal_values(keys[0], (R, 2, BOXES * M), 1.0, 6.0, ((2, 64),))
    radiation = normal_values(keys[1], (2, BOXES, M, K), (2 * M) ** -0.5, 0.5, ((1, 64), (3, 8)))
    interp = normal_values(keys[2], (2, LEVELS, 2, K, SAMP_DEV), (4 * SAMP_DEV) ** -0.5, 0.1875, ((3, 8),))
    translation = jnp.clip(jax.random.uniform(keys[3], (2, TYPES, K), jnp.float32, -1.0, 1.0) * shard_levels(keys[3], (2, TYPES, K), ((2, 8),), -0.4, 0.0), -1.0, 1.0).astype(jnp.bfloat16)
    inter_owner_keys = jax.random.split(jax.random.fold_in(keys[4], 1), BOXES // BOX_DEV)
    inter_owner_turns = jax.random.permutation(jax.random.fold_in(keys[4], 3), BOXES // BOX_DEV)
    inter_owner = jax.vmap(lambda own, number: deal_out(jax.random.fold_in(keys[4], 2), own, number, BOX_DEV, N_BOX, OWN, CAP, 2))(inter_owner_keys, inter_owner_turns).reshape((BOXES, OWN))
    inter_local = touch_ends(jax.random.randint(keys[5], (BOXES, OWN, PER), 0, BOX_DEV), jax.random.fold_in(keys[5], 1), 0, BOX_DEV - 1).astype(jnp.int32)
    inter_type = touch_ends(jax.random.randint(keys[6], (BOXES, OWN, PER), 0, TYPES), jax.random.fold_in(keys[6], 1), 0, TYPES - 1).astype(jnp.int32)
    near_blocks = normal_values(keys[7], (2, NEAR, M, M), (2 * M * NEAR_DEV * N_SAMP // BOX_DEV) ** -0.5, 0.09375, ((1, 512),))
    near_index = draw_near_index(jax.random.fold_in(keys[9], 71), 0)
    return {"currents": currents, "radiation": radiation, "interp": interp, "translation": translation, "inter_owner": inter_owner, "inter_local": inter_local, "inter_type": inter_type, "near_blocks": near_blocks, "near_index": near_index}


def rounded(values):
    return lax.optimization_barrier(values.astype(jnp.bfloat16)).astype(jnp.float32)

def block_product(patterns, weights):
    return jnp.einsum('brik,ikl->bril', patterns, weights)

def near_field(current_grid, near_blocks, near_index):
    group_count = near_index.shape[0] // NEAR_DEV

    def add_group(group, total):
        first = (group * NEAR_DEV).astype(jnp.int32)
        zero_index = jnp.zeros((), jnp.int32)
        blocks = lax.dynamic_slice(near_blocks, (zero_index, first, zero_index, zero_index), (2, NEAR_DEV, M, M)).astype(jnp.float32)
        pairs = lax.dynamic_slice(near_index, (first, zero_index), (NEAR_DEV, 2))
        picked = current_grid[:, :, pairs[:, 1], :]
        real_part = jnp.einsum('nij,rnj->rni', blocks[0], picked[:, 0]) - jnp.einsum('nij,rnj->rni', blocks[1], picked[:, 1])
        imag_part = jnp.einsum('nij,rnj->rni', blocks[0], picked[:, 1]) + jnp.einsum('nij,rnj->rni', blocks[1], picked[:, 0])
        return total.at[:, :, pairs[:, 0], :].add(jnp.stack([real_part, imag_part], axis=1))
    return lax.fori_loop(0, group_count, add_group, jnp.zeros((R, 2, BOXES, M), jnp.float32))

def reference(currents, radiation, interp, translation, inter_owner, inter_local, inter_type, near_blocks, near_index):
    current_grid = currents.astype(jnp.float32).reshape(R, 2, BOXES, M)
    radiation_f = radiation.astype(jnp.float32)
    agg_real = jnp.einsum('bmk,rbm->brk', radiation_f[0], current_grid[:, 0]) - jnp.einsum('bmk,rbm->brk', radiation_f[1], current_grid[:, 1])
    agg_imag = jnp.einsum('bmk,rbm->brk', radiation_f[0], current_grid[:, 1]) + jnp.einsum('bmk,rbm->brk', radiation_f[1], current_grid[:, 0])
    pattern = rounded(jnp.stack([agg_real, agg_imag]))
    for bit_level in range(LEVELS):
        flipped = np.arange(N_SAMP) ^ 1 << bit_level
        blocks = pattern.reshape(2, BOXES, R, N_SAMP, SAMP_DEV)
        partner = blocks[:, :, :, flipped, :]
        weights = interp[:, bit_level].astype(jnp.float32).reshape(2, 2, N_SAMP, SAMP_DEV, SAMP_DEV)
        new_real = block_product(blocks[0], weights[0, 0]) - block_product(blocks[1], weights[1, 0]) + block_product(partner[0], weights[0, 1]) - block_product(partner[1], weights[1, 1])
        new_imag = block_product(blocks[0], weights[1, 0]) + block_product(blocks[1], weights[0, 0]) + block_product(partner[0], weights[1, 1]) + block_product(partner[1], weights[0, 1])
        pattern = rounded(jnp.stack([new_real, new_imag]).reshape(2, BOXES, R, K))
    operators = translation.astype(jnp.float32)
    incoming = jnp.zeros((2, BOXES, R, K), jnp.float32)
    for owner_slot in range(OWN):
        for entry_slot in range(PER):
            target = inter_owner[:, owner_slot] * BOX_DEV + inter_local[:, owner_slot, entry_slot]
            chosen = operators[:, inter_type[:, owner_slot, entry_slot], :]
            part_real = chosen[0][:, None, :] * pattern[0] - chosen[1][:, None, :] * pattern[1]
            part_imag = chosen[0][:, None, :] * pattern[1] + chosen[1][:, None, :] * pattern[0]
            incoming = incoming.at[:, target].add(rounded(jnp.stack([part_real, part_imag])))
    incoming_rounded = rounded(incoming)
    far_scale = math.sqrt(M / (K * OWN * PER))
    far_real = jnp.einsum('bmk,brk->rbm', radiation_f[0], incoming_rounded[0]) + jnp.einsum('bmk,brk->rbm', radiation_f[1], incoming_rounded[1])
    far_imag = jnp.einsum('bmk,brk->rbm', radiation_f[0], incoming_rounded[1]) - jnp.einsum('bmk,brk->rbm', radiation_f[1], incoming_rounded[0])
    far = far_scale * jnp.stack([far_real, far_imag], axis=1)
    near = near_field(current_grid, near_blocks, near_index)
    return (near + far).reshape(R, 2, BOXES * M)
```

```python
import functools
import math

import jax
import jax.numpy as jnp
from jax import lax
from jax.experimental import pallas as pl
from jax.experimental.pallas import tpu as pltpu
from jax.sharding import PartitionSpec as P

M = 64
K = 2048
OWN = 4
PER = 2
TYPES = 316
R = 16
B = 8
S = 256
NEAR = 32
NY, NZ, NC = 4, 8, 2
NS = 8
H = 2
RH = R // H
ROWS = R * 2 * B
HROWS = ROWS // H
LINE = NZ * NC
F32 = jnp.float32
BF16 = jnp.bfloat16
FAR_SCALE = math.sqrt(M / (K * OWN * PER))


def remote(src, dst, send, recv, device):
    return pltpu.make_async_remote_copy(
        src_ref=src,
        dst_ref=dst,
        send_sem=send,
        recv_sem=recv,
        device_id=device,
        device_id_type=pl.DeviceIdType.MESH,
    )


def dot(a, b):
    return jnp.dot(a, b, preferred_element_type=F32)


def dot_nt(a, b):
    return lax.dot_general(a, b, (((1,), (1,)), ((), ())), preferred_element_type=F32)


def kernel(
    cur_h,
    rad_h,
    itp_h,
    trn_h,
    near_h,
    owner_s,
    local_s,
    type_s,
    nidx_s,
    out_ref,
    cur,
    halo,
    rad,
    itp,
    trn,
    nb,
    cur32,
    expanded,
    grid,
    near_y,
    near2d,
    xb,
    yb,
    xg,
    tb,
    tr,
    ops,
    pb,
    hm,
    sb,
    sf,
    yr,
    fs,
    fr,
    in_sem,
    halo_ss,
    halo_rs,
    lev_ss,
    lev_rs,
    tab_ss,
    tab_rs,
    right_ss,
    right_rs,
    left_ss,
    left_rs,
    sib_ss,
    sib_rs,
    y_ss,
    y_rs,
    fin_ss,
    fin_rs,
):
    box = lax.axis_index("box")
    samp = lax.axis_index("samp")
    y = box // LINE
    g = box % LINE
    zl = g // NC
    c = g % NC
    line0 = y * LINE
    sibling = line0 + zl * NC + 1 - c
    zr_dev = (line0 + jnp.minimum(zl + 1, NZ - 1) * NC + c, samp)
    zl_dev = (line0 + jnp.maximum(zl - 1, 0) * NC + c, samp)
    sib_dev = (sibling, samp)
    has_prev = box > 0
    has_next = box < NY * LINE - 1
    prev_dev = (jnp.maximum(box - 1, 0), samp)
    next_dev = (jnp.minimum(box + 1, NY * LINE - 1), samp)
    prev_far = jnp.logical_and(has_prev, g == 0)
    next_far = jnp.logical_and(has_next, g == LINE - 1)

    barrier = pltpu.get_barrier_semaphore()

    def greet(device):
        pl.semaphore_signal(barrier, inc=1, device_id=device, device_id_type=pl.DeviceIdType.MESH)

    for k in range(1, NS):
        greet((box, (samp + k) % NS))
    for k in range(1, LINE):
        greet((line0 + (g + k) % LINE, samp))
    for k in range(1, NY):
        greet(((box + k * LINE) % (NY * LINE), samp))

    @pl.when(prev_far)
    def _():
        greet(prev_dev)

    @pl.when(next_far)
    def _():
        greet(next_dev)

    loads = [
        pltpu.make_async_copy(cur_h, cur, in_sem.at[0]),
        pltpu.make_async_copy(rad_h, rad, in_sem.at[1]),
        pltpu.make_async_copy(itp_h, itp, in_sem.at[2]),
        pltpu.make_async_copy(near_h, nb, in_sem.at[3]),
        pltpu.make_async_copy(trn_h, trn, in_sem.at[4]),
    ]
    for load in loads:
        load.start()

    row = lax.broadcasted_iota(jnp.int32, (128, 128), 0)
    lane8 = lax.broadcasted_iota(jnp.int32, (8, 128), 1)
    row_slot = row % 2
    row_owner = ((row // 2 % NY) * NZ + row // 16) * NC + row // 8 % NC

    def add_box(b, carry):
        value, count = carry
        for j in range(OWN):
            field = jnp.where(
                lane8 == 0,
                b,
                jnp.where(
                    lane8 == 1,
                    type_s[j * PER, b],
                    jnp.where(
                        lane8 == 2,
                        type_s[j * PER + 1, b],
                        jnp.where(
                            lane8 == 3,
                            local_s[j * PER, b],
                            jnp.where(lane8 == 4, local_s[j * PER + 1, b], -1),
                        ),
                    ),
                ),
            )
            hit = row_owner == owner_s[j, b]
            take = jnp.logical_and(hit, count == row_slot)
            wide = jnp.broadcast_to(field[None], (16, 8, 128)).reshape(128, 128)
            value = jnp.where(take, wide, value)
            count = count + jnp.where(hit, 1, 0)
        return value, count

    table, _ = lax.fori_loop(
        0, B, add_box, (jnp.full((128, 128), -1, jnp.int32), jnp.zeros((128, 128), jnp.int32))
    )
    tb[...] = table.reshape(LINE, 8, 128)

    lane_box = lax.broadcasted_iota(jnp.int32, (8, B * M), 1) // M
    own_box = lane_box == lax.broadcasted_iota(jnp.int32, (8, B * M), 0)
    loads[0].wait()

    def widen(src, dst):
        wide = src[...].astype(F32)
        for r in range(R):
            dst[pl.ds(2 * r, 2), :] = wide[r]

    widen(cur, cur32.at[1])
    for r in range(R):
        two = []
        for p in range(2):
            one = jnp.broadcast_to(cur32[1, pl.ds(2 * r + p, 1), :], (8, B * M))
            two.append(jnp.where(own_box, one, 0.0))
        expanded[pl.ds(16 * r, 16), :] = jnp.concatenate(two, axis=0).astype(BF16)

    loads[1].wait()

    def store_pairs(dst, real, imag):
        both = jnp.concatenate([real[:, None], imag[:, None]], axis=1)
        dst[...] = both.reshape(HROWS, S).astype(BF16)

    for h in range(H):
        rows = expanded[pl.ds(h * HROWS, HROWS), :]
        a = dot(rows, rad[0].reshape(B * M, S)).reshape(RH, 2, B, S)
        b = dot(rows, rad[1].reshape(B * M, S)).reshape(RH, 2, B, S)
        store_pairs(xb.at[0, h], a[:, 0] - b[:, 1], a[:, 1] + b[:, 0])

    far_peers = prev_far.astype(jnp.int32) + next_far.astype(jnp.int32)
    pl.semaphore_wait(barrier, NS - 1 + LINE - 1 + NY - 1 + far_peers)

    def level_copy(level, h):
        bit = 1 << level
        partner = samp + bit - 2 * bit * (samp // bit % 2)
        return remote(
            xb.at[level, h], yb.at[level, h], lev_ss.at[level, h], lev_rs.at[level, h], (box, partner)
        )

    for h in range(H):
        level_copy(0, h).start()

    to_next = remote(cur, halo.at[0], halo_ss.at[0], halo_rs.at[0], next_dev)
    to_prev = remote(cur, halo.at[1], halo_ss.at[1], halo_rs.at[1], prev_dev)

    @pl.when(has_next)
    def _():
        to_next.start()

    @pl.when(has_prev)
    def _():
        to_prev.start()

    def table_copy(k):
        to = (g + k) % LINE
        return remote(tb.at[to], tr.at[g], tab_ss.at[k], tab_rs.at[k], (line0 + to, samp))

    for k in range(1, LINE):
        table_copy(k).start()
    tr[g] = tb[g]

    @pl.when(has_prev)
    def _():
        to_next.wait_recv()

    @pl.when(jnp.logical_not(has_prev))
    def _():
        halo[0] = jnp.zeros((R, 2, B * M), BF16)

    @pl.when(has_next)
    def _():
        to_prev.wait_recv()

    @pl.when(jnp.logical_not(has_next))
    def _():
        halo[1] = jnp.zeros((R, 2, B * M), BF16)

    widen(halo.at[0], cur32.at[0])
    widen(halo.at[1], cur32.at[2])
    odd = lax.broadcasted_iota(jnp.int32, (2 * R, B * M), 0) % 2
    for part in range(3):
        plain = cur32[part]
        turned = jnp.where(
            odd == 1, pltpu.roll(plain, 1, 0), -pltpu.roll(plain, 2 * R - 1, 0)
        )
        for b in range(B):
            grid[0, part * B + b] = plain[:, b * M : (b + 1) * M].astype(BF16)
            grid[1, part * B + b] = turned[:, b * M : (b + 1) * M].astype(BF16)
    loads[3].wait()
    first = box * B - B

    def near_one(n, carry):
        source = jnp.clip(nidx_s[1, n] - first, 0, 3 * B - 1)
        near_y[n] = dot_nt(grid[0, source], nb[0, n]) + dot_nt(grid[1, source], nb[1, n])
        return carry

    lax.fori_loop(0, NEAR, near_one, 0, unroll=4)

    def near_add(n, carry):
        target = nidx_s[0, n] - first - B
        value = near_y[n]
        return tuple(
            total + value * jnp.where(target == d, 1.0, 0.0) for d, total in enumerate(carry)
        )

    sums = lax.fori_loop(
        0, NEAR, near_add, tuple(jnp.zeros((2 * R, M), F32) for _ in range(B)), unroll=2
    )
    for q in range(B // 2):
        near2d[q] = jnp.concatenate([sums[2 * q], sums[2 * q + 1]], axis=1)

    loads[2].wait()

    def level_step(level, h, dst):
        own = xb[level, h]
        pair = yb[level, h]
        a = (dot(own, itp[0, level, 0]) + dot(pair, itp[0, level, 1])).reshape(RH, 2, B, S)
        b = (dot(own, itp[1, level, 0]) + dot(pair, itp[1, level, 1])).reshape(RH, 2, B, S)
        store_pairs(dst, a[:, 0] - b[:, 1], a[:, 1] + b[:, 0])

    for h in range(H):
        level_copy(0, h).wait_recv()
        level_step(0, h, xb.at[1, h])
        level_copy(1, h).start()

    for k in range(1, LINE):
        table_copy(k).wait_recv()
    loads[4].wait()
    slots = tr[...]
    flat = slots.reshape(128, 128)
    type_lane = lax.broadcasted_iota(jnp.int32, (128, TYPES), 1)
    lane = lax.broadcasted_iota(jnp.int32, (LINE, 8, 128), 2)
    slot_y = lax.broadcasted_iota(jnp.int32, (LINE, 8, 128), 1) // 2
    hot = []
    for e in range(PER):
        pick = jnp.where(flat[:, 1 + e : 2 + e] == type_lane, 1.0, 0.0).astype(BF16)
        for p in range(2):
            ops[e, p] = dot(pick, trn[p]).reshape(LINE, 8, S)
        good = jnp.logical_and(slots[:, :, 3 + e : 4 + e] == lane % B, lane // B == slot_y)
        hot.append(jnp.where(good, 1.0, 0.0)[:, None])
    spread = jnp.concatenate(hot, axis=1).reshape(2 * 128, 128)
    hm[...] = jnp.transpose(spread)[: NY * B].astype(BF16)

    for h in range(H):
        level_copy(1, h).wait_recv()
        level_step(1, h, xb.at[2, h])
        level_copy(2, h).start()

    def piece(z, core, h):
        return xg.at[z * NC + core, pl.ds(h * HROWS, HROWS)]

    def to_right(z, h):
        return remote(piece(z, c, h), piece(z, c, h), right_ss.at[z, h], right_rs.at[z, h], zr_dev)

    def to_left(z, h):
        return remote(piece(z, c, h), piece(z, c, h), left_ss.at[z, h], left_rs.at[z, h], zl_dev)

    def to_sib(z, h):
        return remote(piece(z, c, h), piece(z, c, h), sib_ss.at[z, h], sib_rs.at[z, h], sib_dev)

    def from_sib(z, h):
        there = piece(z, 1 - c, h)
        return remote(there, there, sib_ss.at[z, h], sib_rs.at[z, h], sib_dev)

    def translate(slot, h):
        index = jnp.broadcast_to(jnp.maximum(tr[slot][:, 0:1], 0), (8, S))
        op = [[ops[e, p, slot] for p in range(2)] for e in range(PER)]
        at = pl.multiple_of(slot * 16, 16)
        for k in range(RH):
            r = h * RH + k
            both = xg[slot, pl.ds(r * 16, 16), :].astype(F32)
            re = jnp.take_along_axis(both[:8], index, axis=0)
            im = jnp.take_along_axis(both[8:], index, axis=0)
            real = [op[e][0] * re - op[e][1] * im for e in range(PER)]
            imag = [op[e][0] * im + op[e][1] * re for e in range(PER)]
            pb[r, 0, pl.ds(at, 16), :] = jnp.concatenate(real, axis=0).astype(BF16)
            pb[r, 1, pl.ds(at, 16), :] = jnp.concatenate(imag, axis=0).astype(BF16)

    for h in range(H):
        level_copy(2, h).wait_recv()
        level_step(2, h, piece(zl, c, h))

        @pl.when(zl < NZ - 1)
        def _():
            to_right(zl, h).start()

        @pl.when(zl > 0)
        def _():
            to_left(zl, h).start()

        to_sib(zl, h).start()

    def sib_slot(z, h):
        from_sib(z, h).wait_recv()
        translate(z * NC + 1 - c, h)

    def distance(d, carry):
        lower = zl - d
        upper = zl + d
        for h in range(H):

            @pl.when(lower >= 0)
            def _():
                to_right(lower, h).wait_recv()

                @pl.when(zl < NZ - 1)
                def _():
                    to_right(lower, h).start()

                to_sib(lower, h).start()

            @pl.when(upper < NZ)
            def _():
                to_left(upper, h).wait_recv()

                @pl.when(zl > 0)
                def _():
                    to_left(upper, h).start()

                to_sib(upper, h).start()

            @pl.when(lower + 1 >= 0)
            def _():
                translate((lower + 1) * NC + c, h)
                sib_slot(lower + 1, h)

            @pl.when(jnp.logical_and(d > 1, upper - 1 < NZ))
            def _():
                translate((upper - 1) * NC + c, h)
                sib_slot(upper - 1, h)

        return carry

    lax.fori_loop(1, NZ + 1, distance, 0)

    def y_copy(k, h):
        to = (y + k) % NY
        part = pl.ds(h * HROWS, HROWS)
        return remote(
            sb.at[to, part], yr.at[y, part], y_ss.at[k, h], y_rs.at[k, h], ((box + k * LINE) % (NY * LINE), samp)
        )

    def fin_copy(s):
        return remote(fs.at[s], fr.at[samp], fin_ss.at[s], fin_rs.at[samp], (box, s))

    weights = hm[...]
    for h in range(H):
        for k in range(RH):
            r = h * RH + k
            real = dot(weights, pb[r, 0])
            imag = dot(weights, pb[r, 1])
            for q in range(NY):
                both = jnp.concatenate([real[q * B : (q + 1) * B], imag[q * B : (q + 1) * B]], axis=0)
                sf[q, pl.ds(r * 16, 16), :] = both
                sb[q, pl.ds(r * 16, 16), :] = both.astype(BF16)
        for k in range(1, NY):
            y_copy(k, h).start()

    for h in range(H):
        part = pl.ds(h * HROWS, HROWS)
        incoming = sf[y, part, :]
        for k in range(1, NY):
            y_copy(NY - k, h).wait_recv()
            incoming = incoming + yr[(y + k) % NY, part, :].astype(F32)
        rounded = incoming.astype(BF16)
        a = dot_nt(rounded, rad[0].reshape(B * M, S)).reshape(RH, 2, B, B * M)
        b = dot_nt(rounded, rad[1].reshape(B * M, S)).reshape(RH, 2, B, B * M)
        far = [a[:, 0] + b[:, 1], a[:, 1] - b[:, 0]]
        for p in range(2):
            picked = jnp.sum(jnp.where(own_box[None], far[p], 0.0), axis=1) * FAR_SCALE
            near = [near2d[q, pl.ds(h * 2 * RH + p, RH, stride=2), :] for q in range(B // 2)]
            total = picked + jnp.concatenate(near, axis=1)
            for k in range(RH):
                r = h * RH + k
                fs[r // 2, pl.ds(r % 2 * 2 + p, 1), :] = total[k : k + 1]
        for s in range(h * NS // H, (h + 1) * NS // H):

            @pl.when(s != samp)
            def _():
                fin_copy(s).start()

    total = fs[samp]
    for k in range(1, NS):
        s = (samp + k) % NS
        there = remote(fs.at[s], fr.at[s], fin_ss.at[s], fin_rs.at[s], (box, s))
        there.wait_recv()
        total = total + fr[s]
    out_ref[0] = total[0:2]
    out_ref[1] = total[2:4]

    for level in range(3):
        for h in range(H):
            level_copy(level, h).wait_send()

    @pl.when(has_next)
    def _():
        to_next.wait_send()

    @pl.when(has_prev)
    def _():
        to_prev.wait_send()

    for k in range(1, LINE):
        table_copy(k).wait_send()
    for k in range(1, NY):
        for h in range(H):
            y_copy(k, h).wait_send()

    def drain(z, carry):
        for h in range(H):

            @pl.when(jnp.logical_and(z <= zl, zl < NZ - 1))
            def _():
                to_right(z, h).wait_send()

            @pl.when(jnp.logical_and(z >= zl, zl > 0))
            def _():
                to_left(z, h).wait_send()

            to_sib(z, h).wait_send()
        return carry

    lax.fori_loop(0, NZ, drain, 0)
    for k in range(1, NS):
        fin_copy((samp + k) % NS).wait_send()


def local(
    currents, radiation, interp, translation, inter_owner, inter_local, inter_type, near_blocks, near_index
):
    hbm = pl.BlockSpec(memory_space=pl.ANY)
    smem = pl.BlockSpec(memory_space=pltpu.SMEM)
    dma = pltpu.SemaphoreType.DMA
    vmem = pltpu.VMEM
    return pl.pallas_call(
        kernel,
        out_shape=jax.ShapeDtypeStruct((2, 2, B * M), F32),
        in_specs=[hbm] * 5 + [smem] * 4,
        out_specs=pl.BlockSpec(memory_space=pltpu.VMEM),
        scratch_shapes=[
            vmem((R, 2, B * M), BF16),
            vmem((2, R, 2, B * M), BF16),
            vmem((2, B, M, S), BF16),
            vmem((2, 3, 2, S, S), BF16),
            vmem((2, TYPES, S), BF16),
            vmem((2, NEAR, M, M), BF16),
            vmem((3, 2 * R, B * M), F32),
            vmem((ROWS, B * M), BF16),
            vmem((2, 3 * B, 2 * R, M), BF16),
            vmem((NEAR, 2 * R, M), F32),
            vmem((B // 2, 2 * R, 2 * M), F32),
            vmem((3, H, HROWS, S), BF16),
            vmem((3, H, HROWS, S), BF16),
            vmem((LINE, ROWS, S), BF16),
            vmem((LINE, 8, 128), jnp.int32),
            vmem((LINE, 8, 128), jnp.int32),
            vmem((PER, 2, LINE, 8, S), F32),
            vmem((R, 2, 2 * 128, S), BF16),
            vmem((NY * B, 2 * 128), BF16),
            vmem((NY, ROWS, S), BF16),
            vmem((NY, ROWS, S), F32),
            vmem((NY, ROWS, S), BF16),
            vmem((NS, 4, B * M), F32),
            vmem((NS, 4, B * M), F32),
            dma((5,)),
            dma((2,)),
            dma((2,)),
            dma((3, H)),
            dma((3, H)),
            dma((LINE,)),
            dma((LINE,)),
            dma((NZ, H)),
            dma((NZ, H)),
            dma((NZ, H)),
            dma((NZ, H)),
            dma((NZ, H)),
            dma((NZ, H)),
            dma((NY, H)),
            dma((NY, H)),
            dma((NS,)),
            dma((NS,)),
        ],
        compiler_params=pltpu.CompilerParams(
            collective_id=0, has_side_effects=True, vmem_limit_bytes=56 * 2**20
        ),
    )(
        currents,
        radiation,
        interp,
        translation,
        near_blocks,
        inter_owner.T,
        jnp.transpose(inter_local, (1, 2, 0)).reshape(OWN * PER, B),
        jnp.transpose(inter_type, (1, 2, 0)).reshape(OWN * PER, B),
        near_index.T,
    )


def solution(mesh):
    in_specs = (
        P(None, None, "box"),
        P(None, "box", None, "samp"),
        P(None, None, None, "samp", None),
        P(None, None, "samp"),
        P("box", None),
        P("box", None, None),
        P("box", None, None),
        P(None, ("box", "samp"), None, None),
        P(("box", "samp"), None),
    )
    return jax.shard_map(local, mesh=mesh, in_specs=in_specs, out_specs=P("samp", None, "box"), check_vma=False)
```

```python
import functools
import math

import jax
import jax.numpy as jnp
from jax import lax
from jax.experimental import pallas as pl
from jax.experimental.pallas import tpu as pltpu
from jax.sharding import PartitionSpec as P

M = 64
K = 2048
OWN = 4
PER = 2
TYPES = 316
TROWS = 640
R = 16
B = 8
S = 256
NEAR = 32
NY, NZ, NC = 4, 8, 2
NS = 8
H = 4
RH = R // H
ROWS = R * 2 * B
HROWS = ROWS // H
Q = 4
RQ = R // Q
QROWS = ROWS // Q
LINE = NZ * NC
F32 = jnp.float32
BF16 = jnp.bfloat16
FAR_SCALE = math.sqrt(M / (K * OWN * PER))


def remote(src, dst, send, recv, device):
    return pltpu.make_async_remote_copy(
        src_ref=src,
        dst_ref=dst,
        send_sem=send,
        recv_sem=recv,
        device_id=device,
        device_id_type=pl.DeviceIdType.MESH,
    )


def dot(a, b):
    return jnp.dot(a, b, preferred_element_type=F32)


def dot_nt(a, b):
    return lax.dot_general(a, b, (((1,), (1,)), ((), ())), preferred_element_type=F32)


def kernel(
    cur_h,
    rad_h,
    itp_h,
    trn_h,
    near_h,
    owner_h,
    local_h,
    type_h,
    nidx_h,
    out_ref,
    owner_s,
    local_s,
    type_s,
    nidx_s,
    cur,
    halo,
    rad,
    itp,
    trn,
    trn32,
    nb,
    cur32,
    expanded,
    grid,
    near_y,
    near2d,
    xb,
    yb,
    xg,
    tb,
    tr,
    ops,
    pb,
    hm,
    sb,
    sf,
    yr,
    fs,
    fr,
    in_sem,
    halo_ss,
    halo_rs,
    lev_ss,
    lev_rs,
    tab_ss,
    tab_rs,
    right_ss,
    right_rs,
    left_ss,
    left_rs,
    sib_ss,
    sib_rs,
    y_ss,
    y_rs,
    fin_ss,
    fin_rs,
):
    box = lax.axis_index("box")
    samp = lax.axis_index("samp")
    y = box // LINE
    g = box % LINE
    zl = g // NC
    c = g % NC
    line0 = y * LINE
    sibling = line0 + zl * NC + 1 - c
    zr_dev = (line0 + jnp.minimum(zl + 1, NZ - 1) * NC + c, samp)
    zl_dev = (line0 + jnp.maximum(zl - 1, 0) * NC + c, samp)
    sib_dev = (sibling, samp)
    has_prev = box > 0
    has_next = box < NY * LINE - 1
    prev_dev = (jnp.maximum(box - 1, 0), samp)
    next_dev = (jnp.minimum(box + 1, NY * LINE - 1), samp)
    prev_far = jnp.logical_and(has_prev, g == 0)
    next_far = jnp.logical_and(has_next, g == LINE - 1)

    barrier = pltpu.get_barrier_semaphore()

    def greet(device):
        pl.semaphore_signal(barrier, inc=1, device_id=device, device_id_type=pl.DeviceIdType.MESH)

    for k in range(1, NS):
        greet((box, (samp + k) % NS))
    for k in range(1, LINE):
        greet((line0 + (g + k) % LINE, samp))
    for k in range(1, NY):
        greet(((box + k * LINE) % (NY * LINE), samp))

    @pl.when(prev_far)
    def _():
        greet(prev_dev)

    @pl.when(next_far)
    def _():
        greet(next_dev)

    loads = [
        pltpu.make_async_copy(cur_h, cur, in_sem.at[0]),
        pltpu.make_async_copy(rad_h, rad, in_sem.at[1]),
        pltpu.make_async_copy(itp_h, itp, in_sem.at[2]),
        pltpu.make_async_copy(near_h, nb, in_sem.at[3]),
        pltpu.make_async_copy(trn_h, trn, in_sem.at[4]),
    ]
    lists = [
        pltpu.make_async_copy(owner_h, owner_s, in_sem.at[5]),
        pltpu.make_async_copy(local_h, local_s, in_sem.at[6]),
        pltpu.make_async_copy(type_h, type_s, in_sem.at[7]),
        pltpu.make_async_copy(nidx_h, nidx_s, in_sem.at[8]),
    ]
    for load in lists:
        load.start()
    for load in loads:
        load.start()

    row = lax.broadcasted_iota(jnp.int32, (128, 128), 0)
    lane8 = lax.broadcasted_iota(jnp.int32, (8, 128), 1)
    row_slot = row % 2
    row_owner = ((row // 2 % NY) * NZ + row // 16) * NC + row // 8 % NC

    for load in lists:
        load.wait()

    def add_box(b, carry):
        value, count = carry
        for j in range(OWN):
            field = jnp.where(
                lane8 == 0,
                b,
                jnp.where(
                    lane8 == 1,
                    type_s[j * PER, b],
                    jnp.where(
                        lane8 == 2,
                        type_s[j * PER + 1, b],
                        jnp.where(
                            lane8 == 3,
                            local_s[j * PER, b],
                            jnp.where(lane8 == 4, local_s[j * PER + 1, b], -1),
                        ),
                    ),
                ),
            )
            hit = row_owner == owner_s[j, b]
            take = jnp.logical_and(hit, count == row_slot)
            wide = jnp.broadcast_to(field[None], (16, 8, 128)).reshape(128, 128)
            value = jnp.where(take, wide, value)
            count = count + jnp.where(hit, 1, 0)
        return value, count

    table, _ = lax.fori_loop(
        0, B, add_box, (jnp.full((128, 128), -1, jnp.int32), jnp.zeros((128, 128), jnp.int32))
    )
    tb[...] = table.reshape(LINE, 8, 128)

    lane_box = lax.broadcasted_iota(jnp.int32, (8, B * M), 1) // M
    own_box = lane_box == lax.broadcasted_iota(jnp.int32, (8, B * M), 0)
    loads[0].wait()

    def widen(src, dst):
        wide = src[...].astype(F32)
        for r in range(R):
            dst[pl.ds(2 * r, 2), :] = wide[r]

    widen(cur, cur32.at[1])
    for r in range(R):
        two = []
        for p in range(2):
            one = jnp.broadcast_to(cur32[1, pl.ds(2 * r + p, 1), :], (8, B * M))
            two.append(jnp.where(own_box, one, 0.0))
        expanded[pl.ds(16 * r, 16), :] = jnp.concatenate(two, axis=0).astype(BF16)

    loads[1].wait()

    def store_pairs(dst, real, imag):
        both = jnp.concatenate([real[:, None], imag[:, None]], axis=1)
        dst[...] = both.reshape(HROWS, S).astype(BF16)

    for h in range(H):
        rows = expanded[pl.ds(h * HROWS, HROWS), :]
        a = dot(rows, rad[0].reshape(B * M, S)).reshape(RH, 2, B, S)
        b = dot(rows, rad[1].reshape(B * M, S)).reshape(RH, 2, B, S)
        store_pairs(xb.at[0, h], a[:, 0] - b[:, 1], a[:, 1] + b[:, 0])

    loads[4].wait()

    def split(k, carry):
        four = trn[pl.ds(k * 4, 4)].astype(F32)
        rows = jnp.concatenate([four[u] for u in range(4)], axis=0)
        trn32[pl.ds(pl.multiple_of(k * 8, 8), 8), :] = rows
        return carry

    lax.fori_loop(0, TYPES // 4, split, 0)
    trn32[pl.ds(2 * TYPES, TROWS - 2 * TYPES), :] = jnp.zeros((TROWS - 2 * TYPES, S), F32)

    far_peers = prev_far.astype(jnp.int32) + next_far.astype(jnp.int32)
    pl.semaphore_wait(barrier, NS - 1 + LINE - 1 + NY - 1 + far_peers)

    def level_copy(level, h):
        bit = 1 << level
        partner = samp + bit - 2 * bit * (samp // bit % 2)
        return remote(
            xb.at[level, h], yb.at[level, h], lev_ss.at[level, h], lev_rs.at[level, h], (box, partner)
        )

    for h in range(H):
        level_copy(0, h).start()

    to_next = remote(cur, halo.at[0], halo_ss.at[0], halo_rs.at[0], next_dev)
    to_prev = remote(cur, halo.at[1], halo_ss.at[1], halo_rs.at[1], prev_dev)

    @pl.when(has_next)
    def _():
        to_next.start()

    @pl.when(has_prev)
    def _():
        to_prev.start()

    def table_copy(k):
        to = (g + k) % LINE
        return remote(tb.at[to], tr.at[g], tab_ss.at[k], tab_rs.at[k], (line0 + to, samp))

    for k in range(1, LINE):
        table_copy(k).start()
    tr[g] = tb[g]

    @pl.when(has_prev)
    def _():
        to_next.wait_recv()

    @pl.when(jnp.logical_not(has_prev))
    def _():
        halo[0] = jnp.zeros((R, 2, B * M), BF16)

    @pl.when(has_next)
    def _():
        to_prev.wait_recv()

    @pl.when(jnp.logical_not(has_next))
    def _():
        halo[1] = jnp.zeros((R, 2, B * M), BF16)

    widen(halo.at[0], cur32.at[0])
    widen(halo.at[1], cur32.at[2])
    odd = lax.broadcasted_iota(jnp.int32, (2 * R, B * M), 0) % 2
    for part in range(3):
        plain = cur32[part]
        turned = jnp.where(
            odd == 1, pltpu.roll(plain, 1, 0), -pltpu.roll(plain, 2 * R - 1, 0)
        )
        for b in range(B):
            grid[0, part * B + b] = plain[:, b * M : (b + 1) * M].astype(BF16)
            grid[1, part * B + b] = turned[:, b * M : (b + 1) * M].astype(BF16)
    loads[3].wait()
    first = box * B - B

    def near_one(n, carry):
        source = jnp.clip(nidx_s[1, n] - first, 0, 3 * B - 1)
        near_y[n] = dot_nt(grid[0, source], nb[0, n]) + dot_nt(grid[1, source], nb[1, n])
        return carry

    lax.fori_loop(0, NEAR, near_one, 0, unroll=4)

    def near_add(n, carry):
        target = nidx_s[0, n] - first - B
        value = near_y[n]
        return tuple(
            total + value * jnp.where(target == d, 1.0, 0.0) for d, total in enumerate(carry)
        )

    sums = lax.fori_loop(
        0, NEAR, near_add, tuple(jnp.zeros((2 * R, M), F32) for _ in range(B)), unroll=2
    )
    for q in range(B // 2):
        near2d[q] = jnp.concatenate([sums[2 * q], sums[2 * q + 1]], axis=1)

    loads[2].wait()

    def level_step(level, h, dst):
        own = xb[level, h]
        pair = yb[level, h]
        a = (dot(own, itp[0, level, 0]) + dot(pair, itp[0, level, 1])).reshape(RH, 2, B, S)
        b = (dot(own, itp[1, level, 0]) + dot(pair, itp[1, level, 1])).reshape(RH, 2, B, S)
        store_pairs(dst, a[:, 0] - b[:, 1], a[:, 1] + b[:, 0])

    for h in range(H):
        level_copy(0, h).wait_recv()
        level_step(0, h, xb.at[1, h])
        level_copy(1, h).start()

    for k in range(1, LINE):
        table_copy(k).wait_recv()
    operators = trn32[...].astype(BF16)
    slots = tr[...]
    flat = slots.reshape(128, 128)
    type_lane = lax.broadcasted_iota(jnp.int32, (128, TROWS), 1)
    lane = lax.broadcasted_iota(jnp.int32, (LINE, 8, 128), 2)
    slot_y = lax.broadcasted_iota(jnp.int32, (LINE, 8, 128), 1) // 2
    hot = []
    for e in range(PER):
        kind = flat[:, 1 + e : 2 + e]
        for p in range(2):
            pick = jnp.where(2 * kind + p == type_lane, 1.0, 0.0).astype(BF16)
            ops[e, p] = dot(pick, operators).reshape(LINE, 8, S)
        good = jnp.logical_and(slots[:, :, 3 + e : 4 + e] == lane % B, lane // B == slot_y)
        hot.append(jnp.where(good, 1.0, 0.0)[:, None])
    spread = jnp.concatenate(hot, axis=1).reshape(2 * 128, 128)
    hm[...] = jnp.transpose(spread)[: NY * B].astype(BF16)

    for h in range(H):
        level_copy(1, h).wait_recv()
        level_step(1, h, xb.at[2, h])
        level_copy(2, h).start()

    def piece(z, core, q):
        return xg.at[z * NC + core, pl.ds(q * QROWS, QROWS)]

    def to_right(z, q):
        return remote(piece(z, c, q), piece(z, c, q), right_ss.at[z, q], right_rs.at[z, q], zr_dev)

    def to_left(z, q):
        return remote(piece(z, c, q), piece(z, c, q), left_ss.at[z, q], left_rs.at[z, q], zl_dev)

    def to_sib(z, q):
        return remote(piece(z, c, q), piece(z, c, q), sib_ss.at[z, q], sib_rs.at[z, q], sib_dev)

    def from_sib(z, q):
        there = piece(z, 1 - c, q)
        return remote(there, there, sib_ss.at[z, q], sib_rs.at[z, q], sib_dev)

    def translate(slot, q):
        index = jnp.broadcast_to(jnp.maximum(tr[slot][:, 0:1], 0), (8, S))
        op = [[ops[e, p, slot] for p in range(2)] for e in range(PER)]
        at = pl.multiple_of(slot * 16, 16)
        for k in range(RQ):
            r = q * RQ + k
            both = xg[slot, pl.ds(r * 16, 16), :].astype(F32)
            re = jnp.take_along_axis(both[:8], index, axis=0)
            im = jnp.take_along_axis(both[8:], index, axis=0)
            real = [op[e][0] * re - op[e][1] * im for e in range(PER)]
            imag = [op[e][0] * im + op[e][1] * re for e in range(PER)]
            pb[r, 0, pl.ds(at, 16), :] = jnp.concatenate(real, axis=0).astype(BF16)
            pb[r, 1, pl.ds(at, 16), :] = jnp.concatenate(imag, axis=0).astype(BF16)

    for h in range(H):
        level_copy(2, h).wait_recv()
        level_step(2, h, xg.at[g, pl.ds(h * HROWS, HROWS)])

        for q in range(h * Q // H, (h + 1) * Q // H):

            @pl.when(zl < NZ - 1)
            def _():
                to_right(zl, q).start()

            @pl.when(zl > 0)
            def _():
                to_left(zl, q).start()

        for q in range(h * Q // H, (h + 1) * Q // H):
            to_sib(zl, q).start()

    def sib_slot(z, q):
        from_sib(z, q).wait_recv()
        translate(z * NC + 1 - c, q)

    def step(d, q):
        lower = zl - d
        upper = zl + d

        @pl.when(lower >= 0)
        def _():
            to_right(lower, q).wait_recv()

            @pl.when(zl < NZ - 1)
            def _():
                to_right(lower, q).start()

            to_sib(lower, q).start()

        @pl.when(upper < NZ)
        def _():
            to_left(upper, q).wait_recv()

            @pl.when(zl > 0)
            def _():
                to_left(upper, q).start()

            to_sib(upper, q).start()

        @pl.when(lower + 1 >= 0)
        def _():
            translate((lower + 1) * NC + c, q)
            sib_slot(lower + 1, q)

        @pl.when(jnp.logical_and(d > 1, upper - 1 < NZ))
        def _():
            translate((upper - 1) * NC + c, q)
            sib_slot(upper - 1, q)

    def distance(d, carry):
        for q in range(Q):
            step(d, q)
        return carry

    lax.fori_loop(1, NZ - 1, distance, 0)

    def y_copy(k, h):
        to = (y + k) % NY
        part = pl.ds(h * HROWS, HROWS)
        return remote(
            sb.at[to, part], yr.at[y, part], y_ss.at[k, h], y_rs.at[k, h], ((box + k * LINE) % (NY * LINE), samp)
        )

    def fin_copy(s):
        return remote(fs.at[s], fr.at[samp], fin_ss.at[s], fin_rs.at[samp], (box, s))

    weights = hm[...]
    for h in range(H):

        def last(d, carry):
            step(d, h)
            return carry

        lax.fori_loop(NZ - 1, NZ + 1, last, 0)
        for k in range(RH):
            r = h * RH + k
            real = dot(weights, pb[r, 0])
            imag = dot(weights, pb[r, 1])
            for q in range(NY):
                both = jnp.concatenate([real[q * B : (q + 1) * B], imag[q * B : (q + 1) * B]], axis=0)
                sf[q, pl.ds(r * 16, 16), :] = both
                sb[q, pl.ds(r * 16, 16), :] = both.astype(BF16)
        for k in range(1, NY):
            y_copy(k, h).start()

    for h in range(H):
        part = pl.ds(h * HROWS, HROWS)
        incoming = sf[y, part, :]
        for k in range(1, NY):
            y_copy(NY - k, h).wait_recv()
            incoming = incoming + yr[(y + k) % NY, part, :].astype(F32)
        rounded = incoming.astype(BF16)
        a = dot_nt(rounded, rad[0].reshape(B * M, S)).reshape(RH, 2, B, B * M)
        b = dot_nt(rounded, rad[1].reshape(B * M, S)).reshape(RH, 2, B, B * M)
        far = [a[:, 0] + b[:, 1], a[:, 1] - b[:, 0]]
        for p in range(2):
            picked = jnp.sum(jnp.where(own_box[None], far[p], 0.0), axis=1) * FAR_SCALE
            near = [near2d[q, pl.ds(h * 2 * RH + p, RH, stride=2), :] for q in range(B // 2)]
            total = picked + jnp.concatenate(near, axis=1)
            for k in range(RH):
                r = h * RH + k
                fs[r // 2, pl.ds(r % 2 * 2 + p, 1), :] = total[k : k + 1]
        for s in range(h * NS // H, (h + 1) * NS // H):

            @pl.when(s != samp)
            def _():
                fin_copy(s).start()

    total = fs[samp]
    for k in range(1, NS):
        s = (samp + k) % NS
        there = remote(fs.at[s], fr.at[s], fin_ss.at[s], fin_rs.at[s], (box, s))
        there.wait_recv()
        total = total + fr[s]
    for r in range(2):
        for q in range(B // 2):
            out_ref[pl.ds(r * B + 2 * q, 2), :] = total[2 * r : 2 * r + 2, q * 2 * M : (q + 1) * 2 * M]

    for level in range(3):
        for h in range(H):
            level_copy(level, h).wait_send()

    @pl.when(has_next)
    def _():
        to_next.wait_send()

    @pl.when(has_prev)
    def _():
        to_prev.wait_send()

    for k in range(1, LINE):
        table_copy(k).wait_send()
    for k in range(1, NY):
        for h in range(H):
            y_copy(k, h).wait_send()

    def drain(z, carry):
        for q in range(Q):

            @pl.when(jnp.logical_and(z <= zl, zl < NZ - 1))
            def _():
                to_right(z, q).wait_send()

            @pl.when(jnp.logical_and(z >= zl, zl > 0))
            def _():
                to_left(z, q).wait_send()

            to_sib(z, q).wait_send()
        return carry

    lax.fori_loop(0, NZ, drain, 0)
    for k in range(1, NS):
        fin_copy((samp + k) % NS).wait_send()


def local(
    currents, radiation, interp, translation, inter_owner, inter_local, inter_type, near_blocks, near_index
):
    hbm = pl.BlockSpec(memory_space=pl.ANY)
    smem = pltpu.SMEM
    dma = pltpu.SemaphoreType.DMA
    vmem = pltpu.VMEM
    rows = pl.pallas_call(
        kernel,
        out_shape=jax.ShapeDtypeStruct((2 * B, 2 * M), F32),
        in_specs=[hbm] * 9,
        out_specs=pl.BlockSpec(memory_space=pltpu.VMEM),
        scratch_shapes=[
            smem((OWN, B), jnp.int32),
            smem((OWN * PER, B), jnp.int32),
            smem((OWN * PER, B), jnp.int32),
            smem((2, NEAR), jnp.int32),
            vmem((R, 2, B * M), BF16),
            vmem((2, R, 2, B * M), BF16),
            vmem((2, B, M, S), BF16),
            vmem((2, 3, 2, S, S), BF16),
            vmem((TYPES, 2, S), BF16),
            vmem((TROWS, S), F32),
            vmem((2, NEAR, M, M), BF16),
            vmem((3, 2 * R, B * M), F32),
            vmem((ROWS, B * M), BF16),
            vmem((2, 3 * B, 2 * R, M), BF16),
            vmem((NEAR, 2 * R, M), F32),
            vmem((B // 2, 2 * R, 2 * M), F32),
            vmem((3, H, HROWS, S), BF16),
            vmem((3, H, HROWS, S), BF16),
            vmem((LINE, ROWS, S), BF16),
            vmem((LINE, 8, 128), jnp.int32),
            vmem((LINE, 8, 128), jnp.int32),
            vmem((PER, 2, LINE, 8, S), F32),
            vmem((R, 2, 2 * 128, S), BF16),
            vmem((NY * B, 2 * 128), BF16),
            vmem((NY, ROWS, S), BF16),
            vmem((NY, ROWS, S), F32),
            vmem((NY, ROWS, S), BF16),
            vmem((NS, 4, B * M), F32),
            vmem((NS, 4, B * M), F32),
            dma((9,)),
            dma((2,)),
            dma((2,)),
            dma((3, H)),
            dma((3, H)),
            dma((LINE,)),
            dma((LINE,)),
            dma((NZ, Q)),
            dma((NZ, Q)),
            dma((NZ, Q)),
            dma((NZ, Q)),
            dma((NZ, Q)),
            dma((NZ, Q)),
            dma((NY, H)),
            dma((NY, H)),
            dma((NS,)),
            dma((NS,)),
        ],
        compiler_params=pltpu.CompilerParams(
            collective_id=0, has_side_effects=True, vmem_limit_bytes=56 * 2**20
        ),
    )(
        currents,
        radiation,
        interp,
        jnp.transpose(translation, (1, 0, 2)),
        near_blocks,
        inter_owner.T,
        jnp.transpose(inter_local, (1, 2, 0)).reshape(OWN * PER, B),
        jnp.transpose(inter_type, (1, 2, 0)).reshape(OWN * PER, B),
        near_index.T,
    )
    return rows.reshape(2, B // 2, 2, 2 * M).transpose(0, 2, 1, 3).reshape(2, 2, B * M)


def solution(mesh):
    in_specs = (
        P(None, None, "box"),
        P(None, "box", None, "samp"),
        P(None, None, None, "samp", None),
        P(None, None, "samp"),
        P("box", None),
        P("box", None, None),
        P("box", None, None),
        P(None, ("box", "samp"), None, None),
        P(("box", "samp"), None),
    )
    return jax.shard_map(local, mesh=mesh, in_specs=in_specs, out_specs=P("samp", None, "box"), check_vma=False)
```

```python
import functools
import math

import jax
import jax.numpy as jnp
from jax import lax
from jax.experimental import pallas as pl
from jax.experimental.pallas import tpu as pltpu
from jax.sharding import PartitionSpec as P

M = 64
K = 2048
OWN = 4
PER = 2
TYPES = 316
TROWS = 640
R = 16
B = 8
S = 256
NEAR = 32
NY, NZ, NC = 4, 8, 2
NS = 8
H = 4
RH = R // H
ROWS = R * 2 * B
HROWS = ROWS // H
Q = 4
RQ = R // Q
QROWS = ROWS // Q
LINE = NZ * NC
F32 = jnp.float32
BF16 = jnp.bfloat16
FAR_SCALE = math.sqrt(M / (K * OWN * PER))


def remote(src, dst, send, recv, device):
    return pltpu.make_async_remote_copy(
        src_ref=src,
        dst_ref=dst,
        send_sem=send,
        recv_sem=recv,
        device_id=device,
        device_id_type=pl.DeviceIdType.MESH,
    )


def dot(a, b):
    return jnp.dot(a, b, preferred_element_type=F32)


def dot_nt(a, b):
    return lax.dot_general(a, b, (((1,), (1,)), ((), ())), preferred_element_type=F32)


def kernel(
    cur_h,
    rad_h,
    itp_h,
    trn_h,
    near_h,
    owner_h,
    local_h,
    type_h,
    nidx_h,
    out_ref,
    owner_s,
    local_s,
    type_s,
    nidx_s,
    cur,
    halo,
    rad,
    itp,
    trn,
    trn32,
    nb,
    cur32,
    expanded,
    grid,
    near_y,
    near2d,
    xb,
    yb,
    xm,
    wp,
    xg,
    tb,
    tr,
    ops,
    pb,
    hm,
    sb,
    sf,
    yr,
    fs,
    fr,
    in_sem,
    halo_ss,
    halo_rs,
    lev_ss,
    lev_rs,
    wt_ss,
    wt_rs,
    tab_ss,
    tab_rs,
    right_ss,
    right_rs,
    left_ss,
    left_rs,
    sib_ss,
    sib_rs,
    y_ss,
    y_rs,
    fin_ss,
    fin_rs,
):
    box = lax.axis_index("box")
    samp = lax.axis_index("samp")
    y = box // LINE
    g = box % LINE
    zl = g // NC
    c = g % NC
    line0 = y * LINE
    sibling = line0 + zl * NC + 1 - c
    zr_dev = (line0 + jnp.minimum(zl + 1, NZ - 1) * NC + c, samp)
    zl_dev = (line0 + jnp.maximum(zl - 1, 0) * NC + c, samp)
    sib_dev = (sibling, samp)
    has_prev = box > 0
    has_next = box < NY * LINE - 1
    prev_dev = (jnp.maximum(box - 1, 0), samp)
    next_dev = (jnp.minimum(box + 1, NY * LINE - 1), samp)
    prev_far = jnp.logical_and(has_prev, g == 0)
    next_far = jnp.logical_and(has_next, g == LINE - 1)

    barrier = pltpu.get_barrier_semaphore()

    def greet(device):
        pl.semaphore_signal(barrier, inc=1, device_id=device, device_id_type=pl.DeviceIdType.MESH)

    for k in range(1, NS):
        greet((box, (samp + k) % NS))
    for k in range(1, LINE):
        greet((line0 + (g + k) % LINE, samp))
    for k in range(1, NY):
        greet(((box + k * LINE) % (NY * LINE), samp))

    @pl.when(prev_far)
    def _():
        greet(prev_dev)

    @pl.when(next_far)
    def _():
        greet(next_dev)

    loads = [
        pltpu.make_async_copy(cur_h, cur, in_sem.at[0]),
        pltpu.make_async_copy(rad_h, rad, in_sem.at[1]),
        pltpu.make_async_copy(itp_h, itp, in_sem.at[2]),
        pltpu.make_async_copy(near_h, nb, in_sem.at[3]),
        pltpu.make_async_copy(trn_h, trn, in_sem.at[4]),
    ]
    lists = [
        pltpu.make_async_copy(owner_h, owner_s, in_sem.at[5]),
        pltpu.make_async_copy(local_h, local_s, in_sem.at[6]),
        pltpu.make_async_copy(type_h, type_s, in_sem.at[7]),
        pltpu.make_async_copy(nidx_h, nidx_s, in_sem.at[8]),
    ]
    for load in lists:
        load.start()
    for load in loads:
        load.start()

    row = lax.broadcasted_iota(jnp.int32, (128, 128), 0)
    lane8 = lax.broadcasted_iota(jnp.int32, (8, 128), 1)
    row_slot = row % 2
    row_owner = ((row // 2 % NY) * NZ + row // 16) * NC + row // 8 % NC

    for load in lists:
        load.wait()

    def add_box(b, carry):
        value, count = carry
        for j in range(OWN):
            field = jnp.where(
                lane8 == 0,
                b,
                jnp.where(
                    lane8 == 1,
                    type_s[j * PER, b],
                    jnp.where(
                        lane8 == 2,
                        type_s[j * PER + 1, b],
                        jnp.where(
                            lane8 == 3,
                            local_s[j * PER, b],
                            jnp.where(lane8 == 4, local_s[j * PER + 1, b], -1),
                        ),
                    ),
                ),
            )
            hit = row_owner == owner_s[j, b]
            take = jnp.logical_and(hit, count == row_slot)
            wide = jnp.broadcast_to(field[None], (16, 8, 128)).reshape(128, 128)
            value = jnp.where(take, wide, value)
            count = count + jnp.where(hit, 1, 0)
        return value, count

    table, _ = lax.fori_loop(
        0, B, add_box, (jnp.full((128, 128), -1, jnp.int32), jnp.zeros((128, 128), jnp.int32))
    )
    tb[...] = table.reshape(LINE, 8, 128)

    lane_box = lax.broadcasted_iota(jnp.int32, (8, B * M), 1) // M
    own_box = lane_box == lax.broadcasted_iota(jnp.int32, (8, B * M), 0)
    loads[0].wait()

    def widen(src, dst):
        wide = src[...].astype(F32)
        for r in range(R):
            dst[pl.ds(2 * r, 2), :] = wide[r]

    widen(cur, cur32.at[1])
    for r in range(R):
        two = []
        for p in range(2):
            one = jnp.broadcast_to(cur32[1, pl.ds(2 * r + p, 1), :], (8, B * M))
            two.append(jnp.where(own_box, one, 0.0))
        expanded[pl.ds(16 * r, 16), :] = jnp.concatenate(two, axis=0).astype(BF16)

    loads[1].wait()

    def store_pairs(dst, real, imag):
        both = jnp.concatenate([real[:, None], imag[:, None]], axis=1)
        dst[...] = both.reshape(HROWS, S).astype(BF16)

    for h in range(H):
        rows = expanded[pl.ds(h * HROWS, HROWS), :]
        a = dot(rows, rad[0].reshape(B * M, S)).reshape(RH, 2, B, S)
        b = dot(rows, rad[1].reshape(B * M, S)).reshape(RH, 2, B, S)
        store_pairs(xb.at[0, h], a[:, 0] - b[:, 1], a[:, 1] + b[:, 0])

    loads[4].wait()

    def split(k, carry):
        four = trn[pl.ds(k * 4, 4)].astype(F32)
        rows = jnp.concatenate([four[u] for u in range(4)], axis=0)
        trn32[pl.ds(pl.multiple_of(k * 8, 8), 8), :] = rows
        return carry

    lax.fori_loop(0, TYPES // 4, split, 0)
    trn32[pl.ds(2 * TYPES, TROWS - 2 * TYPES), :] = jnp.zeros((TROWS - 2 * TYPES, S), F32)

    far_peers = prev_far.astype(jnp.int32) + next_far.astype(jnp.int32)
    pl.semaphore_wait(barrier, NS - 1 + LINE - 1 + NY - 1 + far_peers)

    def flip(bits):
        other = samp
        for bit in (1, 2, 4):
            if bits & bit:
                other = other + bit - 2 * bit * (samp // bit % 2)
        return (box, other)

    def first_copy(h):
        return remote(xb.at[0, h], yb.at[0, h], lev_ss.at[0, h], lev_rs.at[0, h], flip(1))

    def second_copy(k, h):
        return remote(xb.at[1, h], xm.at[k - 1, h], lev_ss.at[k, h], lev_rs.at[k, h], flip(2 * k))

    def weight_copy(p):
        return remote(itp.at[p, 1], wp.at[p], wt_ss.at[p], wt_rs.at[p], flip(4))

    for h in range(H):
        first_copy(h).start()
    loads[2].wait()
    for p in range(2):
        weight_copy(p).start()

    to_next = remote(cur, halo.at[0], halo_ss.at[0], halo_rs.at[0], next_dev)
    to_prev = remote(cur, halo.at[1], halo_ss.at[1], halo_rs.at[1], prev_dev)

    @pl.when(has_next)
    def _():
        to_next.start()

    @pl.when(has_prev)
    def _():
        to_prev.start()

    def table_copy(k):
        to = (g + k) % LINE
        return remote(tb.at[to], tr.at[g], tab_ss.at[k], tab_rs.at[k], (line0 + to, samp))

    for k in range(1, LINE):
        table_copy(k).start()
    tr[g] = tb[g]

    def level_step(own, pair, weight, dst):
        a = (dot(own, weight(0, 0)) + dot(pair, weight(0, 1))).reshape(RH, 2, B, S)
        b = (dot(own, weight(1, 0)) + dot(pair, weight(1, 1))).reshape(RH, 2, B, S)
        store_pairs(dst, a[:, 0] - b[:, 1], a[:, 1] + b[:, 0])

    for h in range(H):
        first_copy(h).wait_recv()
        level_step(xb[0, h], yb[0, h], lambda p, k: itp[p, 0, k], xb.at[1, h])
        for k in (2, 3, 1):
            second_copy(k, h).start()

    @pl.when(has_prev)
    def _():
        to_next.wait_recv()

    @pl.when(jnp.logical_not(has_prev))
    def _():
        halo[0] = jnp.zeros((R, 2, B * M), BF16)

    @pl.when(has_next)
    def _():
        to_prev.wait_recv()

    @pl.when(jnp.logical_not(has_next))
    def _():
        halo[1] = jnp.zeros((R, 2, B * M), BF16)

    widen(halo.at[0], cur32.at[0])
    widen(halo.at[1], cur32.at[2])
    odd = lax.broadcasted_iota(jnp.int32, (2 * R, B * M), 0) % 2
    for part in range(3):
        plain = cur32[part]
        turned = jnp.where(
            odd == 1, pltpu.roll(plain, 1, 0), -pltpu.roll(plain, 2 * R - 1, 0)
        )
        for b in range(B):
            grid[0, part * B + b] = plain[:, b * M : (b + 1) * M].astype(BF16)
            grid[1, part * B + b] = turned[:, b * M : (b + 1) * M].astype(BF16)
    loads[3].wait()
    first = box * B - B

    def near_one(n):
        source = jnp.clip(nidx_s[1, n] - first, 0, 3 * B - 1)
        near_y[n] = dot_nt(grid[0, source], nb[0, n]) + dot_nt(grid[1, source], nb[1, n])

    for k in range(1, LINE):
        table_copy(k).wait_recv()
    operators = trn32[...].astype(BF16)
    slots = tr[...]
    flat = slots.reshape(128, 128)
    type_lane = lax.broadcasted_iota(jnp.int32, (128, TROWS), 1)
    lane = lax.broadcasted_iota(jnp.int32, (LINE, 8, 128), 2)
    slot_y = lax.broadcasted_iota(jnp.int32, (LINE, 8, 128), 1) // 2
    hot = []
    for e in range(PER):
        kind = flat[:, 1 + e : 2 + e]
        for p in range(2):
            pick = jnp.where(2 * kind + p == type_lane, 1.0, 0.0).astype(BF16)
            ops[e, p] = dot(pick, operators).reshape(LINE, 8, S)
        good = jnp.logical_and(slots[:, :, 3 + e : 4 + e] == lane % B, lane // B == slot_y)
        hot.append(jnp.where(good, 1.0, 0.0)[:, None])
    spread = jnp.concatenate(hot, axis=1).reshape(2 * 128, 128)
    hm[...] = jnp.transpose(spread)[: NY * B].astype(BF16)

    def piece(z, core, q):
        return xg.at[z * NC + core, pl.ds(q * QROWS, QROWS)]

    def to_right(z, q):
        return remote(piece(z, c, q), piece(z, c, q), right_ss.at[z, q], right_rs.at[z, q], zr_dev)

    def to_left(z, q):
        return remote(piece(z, c, q), piece(z, c, q), left_ss.at[z, q], left_rs.at[z, q], zl_dev)

    def to_sib(z, q):
        return remote(piece(z, c, q), piece(z, c, q), sib_ss.at[z, q], sib_rs.at[z, q], sib_dev)

    def from_sib(z, q):
        there = piece(z, 1 - c, q)
        return remote(there, there, sib_ss.at[z, q], sib_rs.at[z, q], sib_dev)

    def translate(slot, q):
        index = jnp.broadcast_to(jnp.maximum(tr[slot][:, 0:1], 0), (8, S))
        op = [[ops[e, p, slot] for p in range(2)] for e in range(PER)]
        at = pl.multiple_of(slot * 16, 16)
        for k in range(RQ):
            r = q * RQ + k
            both = xg[slot, pl.ds(r * 16, 16), :].astype(F32)
            re = jnp.take_along_axis(both[:8], index, axis=0)
            im = jnp.take_along_axis(both[8:], index, axis=0)
            real = [op[e][0] * re - op[e][1] * im for e in range(PER)]
            imag = [op[e][0] * im + op[e][1] * re for e in range(PER)]
            pb[r, 0, pl.ds(at, 16), :] = jnp.concatenate(real, axis=0).astype(BF16)
            pb[r, 1, pl.ds(at, 16), :] = jnp.concatenate(imag, axis=0).astype(BF16)

    def own_piece(q):
        for k in range(1, 4):
            second_copy(k, q).wait_recv()
        level_step(xb[1, q], xm[0, q], lambda p, k: itp[p, 1, k], xb.at[2, q])
        level_step(xm[1, q], xm[2, q], lambda p, k: wp[p, k], yb.at[1, q])
        level_step(xb[2, q], yb[1, q], lambda p, k: itp[p, 2, k], xg.at[g, pl.ds(q * QROWS, QROWS)])

        @pl.when(zl < NZ - 1)
        def _():
            to_right(zl, q).start()

        @pl.when(zl > 0)
        def _():
            to_left(zl, q).start()

        to_sib(zl, q).start()

    def sib_slot(z, q):
        from_sib(z, q).wait_recv()
        translate(z * NC + 1 - c, q)

    def step(d, q):
        lower = zl - d
        upper = zl + d

        @pl.when(lower >= 0)
        def _():
            to_right(lower, q).wait_recv()

            @pl.when(zl < NZ - 1)
            def _():
                to_right(lower, q).start()

            to_sib(lower, q).start()

        @pl.when(upper < NZ)
        def _():
            to_left(upper, q).wait_recv()

            @pl.when(zl > 0)
            def _():
                to_left(upper, q).start()

            to_sib(upper, q).start()

        @pl.when(lower + 1 >= 0)
        def _():
            translate((lower + 1) * NC + c, q)
            sib_slot(lower + 1, q)

        @pl.when(jnp.logical_and(d > 1, upper - 1 < NZ))
        def _():
            translate((upper - 1) * NC + c, q)
            sib_slot(upper - 1, q)

    for p in range(2):
        weight_copy(p).wait_recv()
    for q in range(Q):
        own_piece(q)

    def distance(d, carry):
        for q in range(Q):
            step(d, q)
            near_one(4 * (d - 1) + q)
        return carry

    lax.fori_loop(1, NZ - 1, distance, 0)
    for n in range(NEAR - 8, NEAR):
        near_one(n)

    def y_copy(k, h):
        to = (y + k) % NY
        part = pl.ds(h * HROWS, HROWS)
        return remote(
            sb.at[to, part], yr.at[y, part], y_ss.at[k, h], y_rs.at[k, h], ((box + k * LINE) % (NY * LINE), samp)
        )

    def fin_copy(s):
        return remote(fs.at[s], fr.at[samp], fin_ss.at[s], fin_rs.at[samp], (box, s))

    weights = hm[...]

    def finish(h):
        for k in range(RH):
            r = h * RH + k
            real = dot(weights, pb[r, 0])
            imag = dot(weights, pb[r, 1])
            for q in range(NY):
                both = jnp.concatenate([real[q * B : (q + 1) * B], imag[q * B : (q + 1) * B]], axis=0)
                sf[q, pl.ds(r * 16, 16), :] = both
                sb[q, pl.ds(r * 16, 16), :] = both.astype(BF16)
        for k in range(1, NY):
            y_copy(k, h).start()

    for q in range(Q):
        step(NZ - 1, q)
        step(NZ, q)
        finish(q)

    def near_add(n, carry):
        target = nidx_s[0, n] - first - B
        value = near_y[n]
        return tuple(
            total + value * jnp.where(target == d, 1.0, 0.0) for d, total in enumerate(carry)
        )

    sums = lax.fori_loop(
        0, NEAR, near_add, tuple(jnp.zeros((2 * R, M), F32) for _ in range(B)), unroll=2
    )
    for q in range(B // 2):
        near2d[q] = jnp.concatenate([sums[2 * q], sums[2 * q + 1]], axis=1)

    for h in range(H):
        part = pl.ds(h * HROWS, HROWS)
        incoming = sf[y, part, :]
        for k in range(1, NY):
            y_copy(NY - k, h).wait_recv()
            incoming = incoming + yr[(y + k) % NY, part, :].astype(F32)
        rounded = incoming.astype(BF16)
        a = dot_nt(rounded, rad[0].reshape(B * M, S)).reshape(RH, 2, B, B * M)
        b = dot_nt(rounded, rad[1].reshape(B * M, S)).reshape(RH, 2, B, B * M)
        far = [a[:, 0] + b[:, 1], a[:, 1] - b[:, 0]]
        for p in range(2):
            picked = jnp.sum(jnp.where(own_box[None], far[p], 0.0), axis=1) * FAR_SCALE
            near = [near2d[q, pl.ds(h * 2 * RH + p, RH, stride=2), :] for q in range(B // 2)]
            total = picked + jnp.concatenate(near, axis=1)
            for k in range(RH):
                r = h * RH + k
                fs[r // 2, pl.ds(r % 2 * 2 + p, 1), :] = total[k : k + 1]
        for s in range(h * NS // H, (h + 1) * NS // H):

            @pl.when(s != samp)
            def _():
                fin_copy(s).start()

    own = fs[samp]
    others = jnp.zeros((4, B * M), F32)
    for k in range(1, NS):
        s = (samp + k) % NS
        there = remote(fs.at[s], fr.at[s], fin_ss.at[s], fin_rs.at[s], (box, s))
        there.wait_recv()
        others = others + fr[s]
    for half, total in enumerate((own, others)):
        for r in range(2):
            for q in range(B // 2):
                at = pl.ds(r * B + 2 * q, 2)
                out_ref[half, at, :] = total[2 * r : 2 * r + 2, q * 2 * M : (q + 1) * 2 * M]

    for h in range(H):
        first_copy(h).wait_send()
        for k in range(1, 4):
            second_copy(k, h).wait_send()
    for p in range(2):
        weight_copy(p).wait_send()

    @pl.when(has_next)
    def _():
        to_next.wait_send()

    @pl.when(has_prev)
    def _():
        to_prev.wait_send()

    for k in range(1, LINE):
        table_copy(k).wait_send()
    for k in range(1, NY):
        for h in range(H):
            y_copy(k, h).wait_send()

    def drain(z, carry):
        for q in range(Q):

            @pl.when(jnp.logical_and(z <= zl, zl < NZ - 1))
            def _():
                to_right(z, q).wait_send()

            @pl.when(jnp.logical_and(z >= zl, zl > 0))
            def _():
                to_left(z, q).wait_send()

            to_sib(z, q).wait_send()
        return carry

    lax.fori_loop(0, NZ, drain, 0)
    for k in range(1, NS):
        fin_copy((samp + k) % NS).wait_send()


def local(
    currents, radiation, interp, translation, inter_owner, inter_local, inter_type, near_blocks, near_index
):
    hbm = pl.BlockSpec(memory_space=pl.ANY)
    smem = pltpu.SMEM
    dma = pltpu.SemaphoreType.DMA
    vmem = pltpu.VMEM
    rows = pl.pallas_call(
        kernel,
        out_shape=jax.ShapeDtypeStruct((2, 2 * B, 2 * M), F32),
        in_specs=[hbm] * 9,
        out_specs=pl.BlockSpec(memory_space=pltpu.VMEM),
        scratch_shapes=[
            smem((OWN, B), jnp.int32),
            smem((OWN * PER, B), jnp.int32),
            smem((OWN * PER, B), jnp.int32),
            smem((2, NEAR), jnp.int32),
            vmem((R, 2, B * M), BF16),
            vmem((2, R, 2, B * M), BF16),
            vmem((2, B, M, S), BF16),
            vmem((2, 3, 2, S, S), BF16),
            vmem((TYPES, 2, S), BF16),
            vmem((TROWS, S), F32),
            vmem((2, NEAR, M, M), BF16),
            vmem((3, 2 * R, B * M), F32),
            vmem((ROWS, B * M), BF16),
            vmem((2, 3 * B, 2 * R, M), BF16),
            vmem((NEAR, 2 * R, M), F32),
            vmem((B // 2, 2 * R, 2 * M), F32),
            vmem((3, H, HROWS, S), BF16),
            vmem((2, H, HROWS, S), BF16),
            vmem((3, H, HROWS, S), BF16),
            vmem((2, 2, S, S), BF16),
            vmem((LINE, ROWS, S), BF16),
            vmem((LINE, 8, 128), jnp.int32),
            vmem((LINE, 8, 128), jnp.int32),
            vmem((PER, 2, LINE, 8, S), F32),
            vmem((R, 2, 2 * 128, S), BF16),
            vmem((NY * B, 2 * 128), BF16),
            vmem((NY, ROWS, S), BF16),
            vmem((NY, ROWS, S), F32),
            vmem((NY, ROWS, S), BF16),
            vmem((NS, 4, B * M), F32),
            vmem((NS, 4, B * M), F32),
            dma((9,)),
            dma((2,)),
            dma((2,)),
            dma((4, H)),
            dma((4, H)),
            dma((2,)),
            dma((2,)),
            dma((LINE,)),
            dma((LINE,)),
            dma((NZ, Q)),
            dma((NZ, Q)),
            dma((NZ, Q)),
            dma((NZ, Q)),
            dma((NZ, Q)),
            dma((NZ, Q)),
            dma((NY, H)),
            dma((NY, H)),
            dma((NS,)),
            dma((NS,)),
        ],
        compiler_params=pltpu.CompilerParams(
            collective_id=0, has_side_effects=True, vmem_limit_bytes=56 * 2**20
        ),
    )(
        currents,
        radiation,
        interp,
        jnp.transpose(translation, (1, 0, 2)),
        near_blocks,
        inter_owner.T,
        jnp.transpose(inter_local, (1, 2, 0)).reshape(OWN * PER, B),
        jnp.transpose(inter_type, (1, 2, 0)).reshape(OWN * PER, B),
        near_index.T,
    )
    return (rows[0] + rows[1]).reshape(2, B // 2, 2, 2 * M).transpose(0, 2, 1, 3).reshape(2, 2, B * M)


def solution(mesh):
    in_specs = (
        P(None, None, "box"),
        P(None, "box", None, "samp"),
        P(None, None, None, "samp", None),
        P(None, None, "samp"),
        P("box", None),
        P("box", None, None),
        P("box", None, None),
        P(None, ("box", "samp"), None, None),
        P(("box", "samp"), None),
    )
    return jax.shard_map(local, mesh=mesh, in_specs=in_specs, out_specs=P("samp", None, "box"), check_vma=False)
```

```python
import functools
import math

import jax
import jax.numpy as jnp
from jax import lax
from jax.experimental import pallas as pl
from jax.experimental.pallas import tpu as pltpu
from jax.sharding import PartitionSpec as P

M = 64
K = 2048
OWN = 4
PER = 2
TYPES = 316
TROWS = 640
R = 16
B = 8
S = 256
NEAR = 32
NY, NZ, NC = 4, 8, 2
NS = 8
H = 4
RH = R // H
ROWS = R * 2 * B
HROWS = ROWS // H
Q = 4
RQ = R // Q
QROWS = ROWS // Q
LINE = NZ * NC
F32 = jnp.float32
BF16 = jnp.bfloat16
FAR_SCALE = math.sqrt(M / (K * OWN * PER))


def remote(src, dst, send, recv, device):
    return pltpu.make_async_remote_copy(
        src_ref=src,
        dst_ref=dst,
        send_sem=send,
        recv_sem=recv,
        device_id=device,
        device_id_type=pl.DeviceIdType.MESH,
    )


def dot(a, b):
    return jnp.dot(a, b, preferred_element_type=F32)


def dot_nt(a, b):
    return lax.dot_general(a, b, (((1,), (1,)), ((), ())), preferred_element_type=F32)


def kernel(
    cur_h,
    rad_h,
    itp_h,
    trn_h,
    near_h,
    owner_h,
    local_h,
    type_h,
    nidx_h,
    out_ref,
    owner_s,
    local_s,
    type_s,
    nidx_s,
    cur,
    halo,
    rad,
    itp,
    trn,
    trn32,
    nb,
    cur32,
    expanded,
    grid,
    near_y,
    near2d,
    xb,
    yb,
    xm,
    wp,
    xg,
    tb,
    tr,
    ops,
    pb,
    hm,
    sb,
    sf,
    yr,
    fs,
    fr,
    in_sem,
    halo_ss,
    halo_rs,
    lev_ss,
    lev_rs,
    wt_ss,
    wt_rs,
    tab_ss,
    tab_rs,
    right_ss,
    right_rs,
    left_ss,
    left_rs,
    sib_ss,
    sib_rs,
    y_ss,
    y_rs,
    fin_ss,
    fin_rs,
):
    box = lax.axis_index("box")
    samp = lax.axis_index("samp")
    y = box // LINE
    g = box % LINE
    zl = g // NC
    c = g % NC
    line0 = y * LINE
    sibling = line0 + zl * NC + 1 - c
    zr_dev = (line0 + jnp.minimum(zl + 1, NZ - 1) * NC + c, samp)
    zl_dev = (line0 + jnp.maximum(zl - 1, 0) * NC + c, samp)
    sib_dev = (sibling, samp)
    has_prev = box > 0
    has_next = box < NY * LINE - 1
    prev_dev = (jnp.maximum(box - 1, 0), samp)
    next_dev = (jnp.minimum(box + 1, NY * LINE - 1), samp)
    prev_far = jnp.logical_and(has_prev, g == 0)
    next_far = jnp.logical_and(has_next, g == LINE - 1)

    barrier = pltpu.get_barrier_semaphore()

    def greet(device):
        pl.semaphore_signal(barrier, inc=1, device_id=device, device_id_type=pl.DeviceIdType.MESH)

    for k in range(1, NS):
        greet((box, (samp + k) % NS))
    for k in range(1, LINE):
        greet((line0 + (g + k) % LINE, samp))
    for k in range(1, NY):
        greet(((box + k * LINE) % (NY * LINE), samp))

    @pl.when(prev_far)
    def _():
        greet(prev_dev)

    @pl.when(next_far)
    def _():
        greet(next_dev)

    loads = [
        pltpu.make_async_copy(cur_h, cur, in_sem.at[0]),
        pltpu.make_async_copy(rad_h, rad, in_sem.at[1]),
        pltpu.make_async_copy(itp_h, itp, in_sem.at[2]),
        pltpu.make_async_copy(near_h, nb, in_sem.at[3]),
        pltpu.make_async_copy(trn_h, trn, in_sem.at[4]),
    ]
    lists = [
        pltpu.make_async_copy(owner_h, owner_s, in_sem.at[5]),
        pltpu.make_async_copy(local_h, local_s, in_sem.at[6]),
        pltpu.make_async_copy(type_h, type_s, in_sem.at[7]),
        pltpu.make_async_copy(nidx_h, nidx_s, in_sem.at[8]),
    ]
    for load in lists:
        load.start()
    for load in loads:
        load.start()

    row = lax.broadcasted_iota(jnp.int32, (128, 128), 0)
    lane8 = lax.broadcasted_iota(jnp.int32, (8, 128), 1)
    row_slot = row % 2
    row_owner = ((row // 2 % NY) * NZ + row // 16) * NC + row // 8 % NC

    for load in lists:
        load.wait()

    def add_box(b, carry):
        value, count = carry
        for j in range(OWN):
            field = jnp.where(
                lane8 == 0,
                b,
                jnp.where(
                    lane8 == 1,
                    type_s[j * PER, b],
                    jnp.where(
                        lane8 == 2,
                        type_s[j * PER + 1, b],
                        jnp.where(
                            lane8 == 3,
                            local_s[j * PER, b],
                            jnp.where(lane8 == 4, local_s[j * PER + 1, b], -1),
                        ),
                    ),
                ),
            )
            hit = row_owner == owner_s[j, b]
            take = jnp.logical_and(hit, count == row_slot)
            wide = jnp.broadcast_to(field[None], (16, 8, 128)).reshape(128, 128)
            value = jnp.where(take, wide, value)
            count = count + jnp.where(hit, 1, 0)
        return value, count

    table, _ = lax.fori_loop(
        0, B, add_box, (jnp.full((128, 128), -1, jnp.int32), jnp.zeros((128, 128), jnp.int32))
    )
    tb[...] = table.reshape(LINE, 8, 128)

    lane_box = lax.broadcasted_iota(jnp.int32, (8, B * M), 1) // M
    own_box = lane_box == lax.broadcasted_iota(jnp.int32, (8, B * M), 0)
    loads[0].wait()

    def widen(src, dst):
        wide = src[...].astype(F32)
        for r in range(R):
            dst[pl.ds(2 * r, 2), :] = wide[r]

    widen(cur, cur32.at[1])
    for r in range(R):
        two = []
        for p in range(2):
            one = jnp.broadcast_to(cur32[1, pl.ds(2 * r + p, 1), :], (8, B * M))
            two.append(jnp.where(own_box, one, 0.0))
        expanded[pl.ds(16 * r, 16), :] = jnp.concatenate(two, axis=0).astype(BF16)

    loads[1].wait()

    def store_pairs(dst, real, imag):
        both = jnp.concatenate([real[:, None], imag[:, None]], axis=1)
        dst[...] = both.reshape(HROWS, S).astype(BF16)

    for h in range(H):
        rows = expanded[pl.ds(h * HROWS, HROWS), :]
        a = dot(rows, rad[0].reshape(B * M, S)).reshape(RH, 2, B, S)
        b = dot(rows, rad[1].reshape(B * M, S)).reshape(RH, 2, B, S)
        store_pairs(xb.at[0, h], a[:, 0] - b[:, 1], a[:, 1] + b[:, 0])

    loads[4].wait()

    def split(k, carry):
        four = trn[pl.ds(k * 4, 4)].astype(F32)
        rows = jnp.concatenate([four[u] for u in range(4)], axis=0)
        trn32[pl.ds(pl.multiple_of(k * 8, 8), 8), :] = rows
        return carry

    lax.fori_loop(0, TYPES // 4, split, 0)
    trn32[pl.ds(2 * TYPES, TROWS - 2 * TYPES), :] = jnp.zeros((TROWS - 2 * TYPES, S), F32)

    far_peers = prev_far.astype(jnp.int32) + next_far.astype(jnp.int32)
    pl.semaphore_wait(barrier, NS - 1 + LINE - 1 + NY - 1 + far_peers)

    def flip(bits):
        other = samp
        for bit in (1, 2, 4):
            if bits & bit:
                other = other + bit - 2 * bit * (samp // bit % 2)
        return (box, other)

    def first_copy(h):
        return remote(xb.at[0, h], yb.at[0, h], lev_ss.at[0, h], lev_rs.at[0, h], flip(1))

    def second_copy(k, h):
        return remote(xb.at[1, h], xm.at[k - 1, h], lev_ss.at[k, h], lev_rs.at[k, h], flip(2 * k))

    def weight_copy(p):
        return remote(itp.at[p, 1], wp.at[p], wt_ss.at[p], wt_rs.at[p], flip(4))

    for h in range(H):
        first_copy(h).start()
    loads[2].wait()
    for p in range(2):
        weight_copy(p).start()

    to_next = remote(cur, halo.at[0], halo_ss.at[0], halo_rs.at[0], next_dev)
    to_prev = remote(cur, halo.at[1], halo_ss.at[1], halo_rs.at[1], prev_dev)

    @pl.when(has_next)
    def _():
        to_next.start()

    @pl.when(has_prev)
    def _():
        to_prev.start()

    def table_copy(k):
        to = (g + k) % LINE
        return remote(tb.at[to], tr.at[g], tab_ss.at[k], tab_rs.at[k], (line0 + to, samp))

    for k in range(1, LINE):
        table_copy(k).start()
    tr[g] = tb[g]

    def level_step(own, pair, weight, dst):
        a = (dot(own, weight(0, 0)) + dot(pair, weight(0, 1))).reshape(RH, 2, B, S)
        b = (dot(own, weight(1, 0)) + dot(pair, weight(1, 1))).reshape(RH, 2, B, S)
        store_pairs(dst, a[:, 0] - b[:, 1], a[:, 1] + b[:, 0])

    for h in range(H):
        first_copy(h).wait_recv()
        level_step(xb[0, h], yb[0, h], lambda p, k: itp[p, 0, k], xb.at[1, h])
        for k in (2, 3, 1):
            second_copy(k, h).start()

    @pl.when(has_prev)
    def _():
        to_next.wait_recv()

    @pl.when(jnp.logical_not(has_prev))
    def _():
        halo[0] = jnp.zeros((R, 2, B * M), BF16)

    @pl.when(has_next)
    def _():
        to_prev.wait_recv()

    @pl.when(jnp.logical_not(has_next))
    def _():
        halo[1] = jnp.zeros((R, 2, B * M), BF16)

    widen(halo.at[0], cur32.at[0])
    widen(halo.at[1], cur32.at[2])
    odd = lax.broadcasted_iota(jnp.int32, (2 * R, B * M), 0) % 2
    for part in range(3):
        plain = cur32[part]
        turned = jnp.where(
            odd == 1, pltpu.roll(plain, 1, 0), -pltpu.roll(plain, 2 * R - 1, 0)
        )
        for b in range(B):
            grid[0, part * B + b] = plain[:, b * M : (b + 1) * M].astype(BF16)
            grid[1, part * B + b] = turned[:, b * M : (b + 1) * M].astype(BF16)
    loads[3].wait()
    first = box * B - B

    def near_one(n):
        source = jnp.clip(nidx_s[1, n] - first, 0, 3 * B - 1)
        near_y[n] = dot_nt(grid[0, source], nb[0, n]) + dot_nt(grid[1, source], nb[1, n])

    for k in range(1, LINE):
        table_copy(k).wait_recv()
    operators = trn32[...].astype(BF16)
    slots = tr[...]
    flat = slots.reshape(128, 128)
    type_lane = lax.broadcasted_iota(jnp.int32, (128, TROWS), 1)
    lane = lax.broadcasted_iota(jnp.int32, (LINE, 8, 128), 2)
    slot_y = lax.broadcasted_iota(jnp.int32, (LINE, 8, 128), 1) // 2
    hot = []
    for e in range(PER):
        kind = flat[:, 1 + e : 2 + e]
        for p in range(2):
            pick = jnp.where(2 * kind + p == type_lane, 1.0, 0.0).astype(BF16)
            ops[e, p] = dot(pick, operators).reshape(LINE, 8, S)
        good = jnp.logical_and(slots[:, :, 3 + e : 4 + e] == lane % B, lane // B == slot_y)
        hot.append(jnp.where(good, 1.0, 0.0)[:, None])
    spread = jnp.concatenate(hot, axis=1).reshape(2 * 128, 128)
    hm[...] = jnp.transpose(spread)[: NY * B].astype(BF16)

    def piece(z, core, q):
        return xg.at[z * NC + core, pl.ds(q * QROWS, QROWS)]

    def to_right(z, q):
        return remote(piece(z, c, q), piece(z, c, q), right_ss.at[z, q], right_rs.at[z, q], zr_dev)

    def to_left(z, q):
        return remote(piece(z, c, q), piece(z, c, q), left_ss.at[z, q], left_rs.at[z, q], zl_dev)

    def to_sib(z, q):
        return remote(piece(z, c, q), piece(z, c, q), sib_ss.at[z, q], sib_rs.at[z, q], sib_dev)

    def from_sib(z, q):
        there = piece(z, 1 - c, q)
        return remote(there, there, sib_ss.at[z, q], sib_rs.at[z, q], sib_dev)

    def translate(slot, q):
        index = jnp.broadcast_to(jnp.maximum(tr[slot][:, 0:1], 0), (8, S))
        op = [[ops[e, p, slot] for p in range(2)] for e in range(PER)]
        at = pl.multiple_of(slot * 16, 16)
        for k in range(RQ):
            r = q * RQ + k
            both = xg[slot, pl.ds(r * 16, 16), :].astype(F32)
            re = jnp.take_along_axis(both[:8], index, axis=0)
            im = jnp.take_along_axis(both[8:], index, axis=0)
            real = [op[e][0] * re - op[e][1] * im for e in range(PER)]
            imag = [op[e][0] * im + op[e][1] * re for e in range(PER)]
            pb[r, 0, pl.ds(at, 16), :] = jnp.concatenate(real, axis=0).astype(BF16)
            pb[r, 1, pl.ds(at, 16), :] = jnp.concatenate(imag, axis=0).astype(BF16)

    def own_piece(q):
        for k in range(1, 4):
            second_copy(k, q).wait_recv()
        level_step(xb[1, q], xm[0, q], lambda p, k: itp[p, 1, k], xb.at[2, q])
        level_step(xm[1, q], xm[2, q], lambda p, k: wp[p, k], yb.at[1, q])
        level_step(xb[2, q], yb[1, q], lambda p, k: itp[p, 2, k], xg.at[g, pl.ds(q * QROWS, QROWS)])

        @pl.when(zl < NZ - 1)
        def _():
            to_right(zl, q).start()

        @pl.when(zl > 0)
        def _():
            to_left(zl, q).start()

        to_sib(zl, q).start()

    def sib_slot(z, q):
        from_sib(z, q).wait_recv()
        translate(z * NC + 1 - c, q)

    def step(d, q):
        lower = zl - d
        upper = zl + d

        @pl.when(lower >= 0)
        def _():
            to_right(lower, q).wait_recv()

            @pl.when(zl < NZ - 1)
            def _():
                to_right(lower, q).start()

            to_sib(lower, q).start()

        @pl.when(upper < NZ)
        def _():
            to_left(upper, q).wait_recv()

            @pl.when(zl > 0)
            def _():
                to_left(upper, q).start()

            to_sib(upper, q).start()

        @pl.when(lower + 1 >= 0)
        def _():
            translate((lower + 1) * NC + c, q)
            sib_slot(lower + 1, q)

        @pl.when(jnp.logical_and(d > 1, upper - 1 < NZ))
        def _():
            translate((upper - 1) * NC + c, q)
            sib_slot(upper - 1, q)

    for p in range(2):
        weight_copy(p).wait_recv()
    for q in range(Q):
        own_piece(q)

    def distance(d, carry):
        for q in range(Q):
            step(d, q)
            near_one(4 * (d - 1) + q)
        return carry

    lax.fori_loop(1, NZ - 1, distance, 0)
    for n in range(NEAR - 8, NEAR):
        near_one(n)

    def y_copy(k, h):
        to = (y + k) % NY
        part = pl.ds(h * HROWS, HROWS)
        return remote(
            sb.at[to, part], yr.at[y, part], y_ss.at[k, h], y_rs.at[k, h], ((box + k * LINE) % (NY * LINE), samp)
        )

    def fin_copy(s):
        return remote(fs.at[s], fr.at[samp], fin_ss.at[s], fin_rs.at[samp], (box, s))

    weights = hm[...]

    def finish(h):
        for k in range(RH):
            r = h * RH + k
            real = dot(weights, pb[r, 0])
            imag = dot(weights, pb[r, 1])
            for q in range(NY):
                both = jnp.concatenate([real[q * B : (q + 1) * B], imag[q * B : (q + 1) * B]], axis=0)
                sf[q, pl.ds(r * 16, 16), :] = both
                sb[q, pl.ds(r * 16, 16), :] = both.astype(BF16)
        for k in range(1, NY):
            y_copy(k, h).start()

    for q in range(Q):
        step(NZ - 1, q)
        step(NZ, q)
        finish(q)

    def near_add(n, carry):
        target = nidx_s[0, n] - first - B
        value = near_y[n]
        return tuple(
            total + value * jnp.where(target == d, 1.0, 0.0) for d, total in enumerate(carry)
        )

    sums = lax.fori_loop(
        0, NEAR, near_add, tuple(jnp.zeros((2 * R, M), F32) for _ in range(B)), unroll=2
    )
    for q in range(B // 2):
        near2d[q] = jnp.concatenate([sums[2 * q], sums[2 * q + 1]], axis=1)

    for h in range(H):
        part = pl.ds(h * HROWS, HROWS)
        incoming = sf[y, part, :]
        for k in range(1, NY):
            y_copy(NY - k, h).wait_recv()
            incoming = incoming + yr[(y + k) % NY, part, :].astype(F32)
        rounded = incoming.astype(BF16)
        a = dot_nt(rounded, rad[0].reshape(B * M, S)).reshape(RH, 2, B, B * M)
        b = dot_nt(rounded, rad[1].reshape(B * M, S)).reshape(RH, 2, B, B * M)
        far = [a[:, 0] + b[:, 1], a[:, 1] - b[:, 0]]
        for p in range(2):
            picked = jnp.sum(jnp.where(own_box[None], far[p], 0.0), axis=1) * FAR_SCALE
            near = [near2d[q, pl.ds(h * 2 * RH + p, RH, stride=2), :] for q in range(B // 2)]
            total = picked + jnp.concatenate(near, axis=1)
            for k in range(RH):
                r = h * RH + k
                fs[r // 2, pl.ds(r % 2 * 2 + p, 1), :] = total[k : k + 1]
        for s in range(h * NS // H, (h + 1) * NS // H):

            @pl.when(s != samp)
            def _():
                fin_copy(s).start()

    for h in range(H):
        first_copy(h).wait_send()
        for k in range(1, 4):
            second_copy(k, h).wait_send()
    for p in range(2):
        weight_copy(p).wait_send()

    @pl.when(has_next)
    def _():
        to_next.wait_send()

    @pl.when(has_prev)
    def _():
        to_prev.wait_send()

    for k in range(1, LINE):
        table_copy(k).wait_send()
    for k in range(1, NY):
        for h in range(H):
            y_copy(k, h).wait_send()

    def drain(z, carry):
        for q in range(Q):

            @pl.when(jnp.logical_and(z <= zl, zl < NZ - 1))
            def _():
                to_right(z, q).wait_send()

            @pl.when(jnp.logical_and(z >= zl, zl > 0))
            def _():
                to_left(z, q).wait_send()

            to_sib(z, q).wait_send()
        return carry

    lax.fori_loop(0, NZ, drain, 0)
    own = fs[samp]
    others = jnp.zeros((4, B * M), F32)
    for k in range(1, NS):
        s = (samp + k) % NS
        there = remote(fs.at[s], fr.at[s], fin_ss.at[s], fin_rs.at[s], (box, s))
        there.wait_recv()
        others = others + fr[s]
    for half, total in enumerate((own, others)):
        for r in range(2):
            for q in range(B // 2):
                at = pl.ds(r * B + 2 * q, 2)
                out_ref[half, at, :] = total[2 * r : 2 * r + 2, q * 2 * M : (q + 1) * 2 * M]

    for k in range(1, NS):
        fin_copy((samp + k) % NS).wait_send()


def local(
    currents, radiation, interp, translation, inter_owner, inter_local, inter_type, near_blocks, near_index
):
    hbm = pl.BlockSpec(memory_space=pl.ANY)
    smem = pltpu.SMEM
    dma = pltpu.SemaphoreType.DMA
    vmem = pltpu.VMEM
    rows = pl.pallas_call(
        kernel,
        out_shape=jax.ShapeDtypeStruct((2, 2 * B, 2 * M), F32),
        in_specs=[hbm] * 9,
        out_specs=pl.BlockSpec(memory_space=pltpu.VMEM),
        scratch_shapes=[
            smem((OWN, B), jnp.int32),
            smem((OWN * PER, B), jnp.int32),
            smem((OWN * PER, B), jnp.int32),
            smem((2, NEAR), jnp.int32),
            vmem((R, 2, B * M), BF16),
            vmem((2, R, 2, B * M), BF16),
            vmem((2, B, M, S), BF16),
            vmem((2, 3, 2, S, S), BF16),
            vmem((TYPES, 2, S), BF16),
            vmem((TROWS, S), F32),
            vmem((2, NEAR, M, M), BF16),
            vmem((3, 2 * R, B * M), F32),
            vmem((ROWS, B * M), BF16),
            vmem((2, 3 * B, 2 * R, M), BF16),
            vmem((NEAR, 2 * R, M), F32),
            vmem((B // 2, 2 * R, 2 * M), F32),
            vmem((3, H, HROWS, S), BF16),
            vmem((2, H, HROWS, S), BF16),
            vmem((3, H, HROWS, S), BF16),
            vmem((2, 2, S, S), BF16),
            vmem((LINE, ROWS, S), BF16),
            vmem((LINE, 8, 128), jnp.int32),
            vmem((LINE, 8, 128), jnp.int32),
            vmem((PER, 2, LINE, 8, S), F32),
            vmem((R, 2, 2 * 128, S), BF16),
            vmem((NY * B, 2 * 128), BF16),
            vmem((NY, ROWS, S), BF16),
            vmem((NY, ROWS, S), F32),
            vmem((NY, ROWS, S), BF16),
            vmem((NS, 4, B * M), F32),
            vmem((NS, 4, B * M), F32),
            dma((9,)),
            dma((2,)),
            dma((2,)),
            dma((4, H)),
            dma((4, H)),
            dma((2,)),
            dma((2,)),
            dma((LINE,)),
            dma((LINE,)),
            dma((NZ, Q)),
            dma((NZ, Q)),
            dma((NZ, Q)),
            dma((NZ, Q)),
            dma((NZ, Q)),
            dma((NZ, Q)),
            dma((NY, H)),
            dma((NY, H)),
            dma((NS,)),
            dma((NS,)),
        ],
        compiler_params=pltpu.CompilerParams(
            collective_id=0, has_side_effects=True, vmem_limit_bytes=56 * 2**20
        ),
    )(
        currents,
        radiation,
        interp,
        jnp.transpose(translation, (1, 0, 2)),
        near_blocks,
        inter_owner.T,
        jnp.transpose(inter_local, (1, 2, 0)).reshape(OWN * PER, B),
        jnp.transpose(inter_type, (1, 2, 0)).reshape(OWN * PER, B),
        near_index.T,
    )
    return (rows[0] + rows[1]).reshape(2, B // 2, 2, 2 * M).transpose(0, 2, 1, 3).reshape(2, 2, B * M)


def solution(mesh):
    in_specs = (
        P(None, None, "box"),
        P(None, "box", None, "samp"),
        P(None, None, None, "samp", None),
        P(None, None, "samp"),
        P("box", None),
        P("box", None, None),
        P("box", None, None),
        P(None, ("box", "samp"), None, None),
        P(("box", "samp"), None),
    )
    return jax.shard_map(local, mesh=mesh, in_specs=in_specs, out_specs=P("samp", None, "box"), check_vma=False)
```

```python
import functools
import math

import jax
import jax.numpy as jnp
from jax import lax
from jax.experimental import pallas as pl
from jax.experimental.pallas import tpu as pltpu
from jax.sharding import PartitionSpec as P

M = 64
K = 2048
OWN = 4
PER = 2
TYPES = 316
TROWS = 640
R = 16
B = 8
S = 256
NEAR = 32
NY, NZ, NC = 4, 8, 2
NS = 8
H = 4
RH = R // H
ROWS = R * 2 * B
HROWS = ROWS // H
Q = 4
RQ = R // Q
QROWS = ROWS // Q
LINE = NZ * NC
F32 = jnp.float32
BF16 = jnp.bfloat16
FAR_SCALE = math.sqrt(M / (K * OWN * PER))


def remote(src, dst, send, recv, device):
    return pltpu.make_async_remote_copy(
        src_ref=src,
        dst_ref=dst,
        send_sem=send,
        recv_sem=recv,
        device_id=device,
        device_id_type=pl.DeviceIdType.MESH,
    )


def dot(a, b):
    return jnp.dot(a, b, preferred_element_type=F32)


def dot_nt(a, b):
    return lax.dot_general(a, b, (((1,), (1,)), ((), ())), preferred_element_type=F32)


def kernel(
    cur_h,
    rad_h,
    itp_h,
    trn_h,
    near_h,
    owner_h,
    local_h,
    type_h,
    nidx_h,
    out_ref,
    owner_s,
    local_s,
    type_s,
    nidx_s,
    cur,
    halo,
    rad,
    itp,
    trn,
    trn32,
    nb,
    cur32,
    expanded,
    grid,
    near_y,
    near2d,
    xb,
    yb,
    xm,
    wp,
    xg,
    tb,
    tr,
    ops,
    pb,
    hm,
    sb,
    sf,
    yr,
    fs,
    fb,
    fr,
    in_sem,
    halo_ss,
    halo_rs,
    lev_ss,
    lev_rs,
    wt_ss,
    wt_rs,
    tab_ss,
    tab_rs,
    right_ss,
    right_rs,
    left_ss,
    left_rs,
    sib_ss,
    sib_rs,
    y_ss,
    y_rs,
    fin_ss,
    fin_rs,
):
    box = lax.axis_index("box")
    samp = lax.axis_index("samp")
    y = box // LINE
    g = box % LINE
    zl = g // NC
    c = g % NC
    line0 = y * LINE
    sibling = line0 + zl * NC + 1 - c
    zr_dev = (line0 + jnp.minimum(zl + 1, NZ - 1) * NC + c, samp)
    zl_dev = (line0 + jnp.maximum(zl - 1, 0) * NC + c, samp)
    sib_dev = (sibling, samp)
    has_prev = box > 0
    has_next = box < NY * LINE - 1
    prev_dev = (jnp.maximum(box - 1, 0), samp)
    next_dev = (jnp.minimum(box + 1, NY * LINE - 1), samp)
    prev_far = jnp.logical_and(has_prev, g == 0)
    next_far = jnp.logical_and(has_next, g == LINE - 1)

    barrier = pltpu.get_barrier_semaphore()

    def greet(device):
        pl.semaphore_signal(barrier, inc=1, device_id=device, device_id_type=pl.DeviceIdType.MESH)

    for k in range(1, NS):
        greet((box, (samp + k) % NS))
    for k in range(1, LINE):
        greet((line0 + (g + k) % LINE, samp))
    for k in range(1, NY):
        greet(((box + k * LINE) % (NY * LINE), samp))

    @pl.when(prev_far)
    def _():
        greet(prev_dev)

    @pl.when(next_far)
    def _():
        greet(next_dev)

    loads = [
        pltpu.make_async_copy(cur_h, cur, in_sem.at[0]),
        pltpu.make_async_copy(rad_h, rad, in_sem.at[1]),
        pltpu.make_async_copy(itp_h, itp, in_sem.at[2]),
        pltpu.make_async_copy(near_h, nb, in_sem.at[3]),
        pltpu.make_async_copy(trn_h, trn, in_sem.at[4]),
    ]
    lists = [
        pltpu.make_async_copy(owner_h, owner_s, in_sem.at[5]),
        pltpu.make_async_copy(local_h, local_s, in_sem.at[6]),
        pltpu.make_async_copy(type_h, type_s, in_sem.at[7]),
        pltpu.make_async_copy(nidx_h, nidx_s, in_sem.at[8]),
    ]
    for load in lists:
        load.start()
    for load in loads:
        load.start()

    row = lax.broadcasted_iota(jnp.int32, (128, 128), 0)
    lane8 = lax.broadcasted_iota(jnp.int32, (8, 128), 1)
    row_slot = row % 2
    row_owner = ((row // 2 % NY) * NZ + row // 16) * NC + row // 8 % NC

    for load in lists:
        load.wait()

    def add_box(b, carry):
        value, count = carry
        for j in range(OWN):
            field = jnp.where(
                lane8 == 0,
                b,
                jnp.where(
                    lane8 == 1,
                    type_s[j * PER, b],
                    jnp.where(
                        lane8 == 2,
                        type_s[j * PER + 1, b],
                        jnp.where(
                            lane8 == 3,
                            local_s[j * PER, b],
                            jnp.where(lane8 == 4, local_s[j * PER + 1, b], -1),
                        ),
                    ),
                ),
            )
            hit = row_owner == owner_s[j, b]
            take = jnp.logical_and(hit, count == row_slot)
            wide = jnp.broadcast_to(field[None], (16, 8, 128)).reshape(128, 128)
            value = jnp.where(take, wide, value)
            count = count + jnp.where(hit, 1, 0)
        return value, count

    table, _ = lax.fori_loop(
        0, B, add_box, (jnp.full((128, 128), -1, jnp.int32), jnp.zeros((128, 128), jnp.int32))
    )
    tb[...] = table.reshape(LINE, 8, 128)

    lane_box = lax.broadcasted_iota(jnp.int32, (8, B * M), 1) // M
    own_box = lane_box == lax.broadcasted_iota(jnp.int32, (8, B * M), 0)
    loads[0].wait()

    def widen(src, dst):
        wide = src[...].astype(F32)
        for r in range(R):
            dst[pl.ds(2 * r, 2), :] = wide[r]

    widen(cur, cur32.at[1])
    for r in range(R):
        two = []
        for p in range(2):
            one = jnp.broadcast_to(cur32[1, pl.ds(2 * r + p, 1), :], (8, B * M))
            two.append(jnp.where(own_box, one, 0.0))
        expanded[pl.ds(16 * r, 16), :] = jnp.concatenate(two, axis=0).astype(BF16)

    loads[1].wait()

    def store_pairs(dst, real, imag):
        both = jnp.concatenate([real[:, None], imag[:, None]], axis=1)
        dst[...] = both.reshape(HROWS, S).astype(BF16)

    for h in range(H):
        rows = expanded[pl.ds(h * HROWS, HROWS), :]
        a = dot(rows, rad[0].reshape(B * M, S)).reshape(RH, 2, B, S)
        b = dot(rows, rad[1].reshape(B * M, S)).reshape(RH, 2, B, S)
        store_pairs(xb.at[0, h], a[:, 0] - b[:, 1], a[:, 1] + b[:, 0])

    loads[4].wait()

    def split(k, carry):
        four = trn[pl.ds(k * 4, 4)].astype(F32)
        rows = jnp.concatenate([four[u] for u in range(4)], axis=0)
        trn32[pl.ds(pl.multiple_of(k * 8, 8), 8), :] = rows
        return carry

    lax.fori_loop(0, TYPES // 4, split, 0)
    trn32[pl.ds(2 * TYPES, TROWS - 2 * TYPES), :] = jnp.zeros((TROWS - 2 * TYPES, S), F32)

    far_peers = prev_far.astype(jnp.int32) + next_far.astype(jnp.int32)
    pl.semaphore_wait(barrier, NS - 1 + LINE - 1 + NY - 1 + far_peers)

    def flip(bits):
        other = samp
        for bit in (1, 2, 4):
            if bits & bit:
                other = other + bit - 2 * bit * (samp // bit % 2)
        return (box, other)

    def first_copy(h):
        return remote(xb.at[0, h], yb.at[0, h], lev_ss.at[0, h], lev_rs.at[0, h], flip(1))

    def second_copy(k, h):
        return remote(xb.at[1, h], xm.at[k - 1, h], lev_ss.at[k, h], lev_rs.at[k, h], flip(2 * k))

    def weight_copy(p):
        return remote(itp.at[p, 1], wp.at[p], wt_ss.at[p], wt_rs.at[p], flip(4))

    for h in range(H):
        first_copy(h).start()
    loads[2].wait()
    for p in range(2):
        weight_copy(p).start()

    to_next = remote(cur, halo.at[0], halo_ss.at[0], halo_rs.at[0], next_dev)
    to_prev = remote(cur, halo.at[1], halo_ss.at[1], halo_rs.at[1], prev_dev)

    @pl.when(has_next)
    def _():
        to_next.start()

    @pl.when(has_prev)
    def _():
        to_prev.start()

    def table_copy(k):
        to = (g + k) % LINE
        return remote(tb.at[to], tr.at[g], tab_ss.at[k], tab_rs.at[k], (line0 + to, samp))

    for k in range(1, LINE):
        table_copy(k).start()
    tr[g] = tb[g]

    def level_step(own, pair, weight, dst):
        a = (dot(own, weight(0, 0)) + dot(pair, weight(0, 1))).reshape(RH, 2, B, S)
        b = (dot(own, weight(1, 0)) + dot(pair, weight(1, 1))).reshape(RH, 2, B, S)
        store_pairs(dst, a[:, 0] - b[:, 1], a[:, 1] + b[:, 0])

    for h in range(H):
        first_copy(h).wait_recv()
        level_step(xb[0, h], yb[0, h], lambda p, k: itp[p, 0, k], xb.at[1, h])
        for k in (2, 3, 1):
            second_copy(k, h).start()

    @pl.when(has_prev)
    def _():
        to_next.wait_recv()

    @pl.when(jnp.logical_not(has_prev))
    def _():
        halo[0] = jnp.zeros((R, 2, B * M), BF16)

    @pl.when(has_next)
    def _():
        to_prev.wait_recv()

    @pl.when(jnp.logical_not(has_next))
    def _():
        halo[1] = jnp.zeros((R, 2, B * M), BF16)

    widen(halo.at[0], cur32.at[0])
    widen(halo.at[1], cur32.at[2])
    odd = lax.broadcasted_iota(jnp.int32, (2 * R, B * M), 0) % 2
    for part in range(3):
        plain = cur32[part]
        turned = jnp.where(
            odd == 1, pltpu.roll(plain, 1, 0), -pltpu.roll(plain, 2 * R - 1, 0)
        )
        for b in range(B):
            grid[0, part * B + b] = plain[:, b * M : (b + 1) * M].astype(BF16)
            grid[1, part * B + b] = turned[:, b * M : (b + 1) * M].astype(BF16)
    loads[3].wait()
    first = box * B - B

    def near_one(n):
        source = jnp.clip(nidx_s[1, n] - first, 0, 3 * B - 1)
        near_y[n] = dot_nt(grid[0, source], nb[0, n]) + dot_nt(grid[1, source], nb[1, n])

    for k in range(1, LINE):
        table_copy(k).wait_recv()
    operators = trn32[...].astype(BF16)
    slots = tr[...]
    flat = slots.reshape(128, 128)
    type_lane = lax.broadcasted_iota(jnp.int32, (128, TROWS), 1)
    lane = lax.broadcasted_iota(jnp.int32, (LINE, 8, 128), 2)
    slot_y = lax.broadcasted_iota(jnp.int32, (LINE, 8, 128), 1) // 2
    hot = []
    for e in range(PER):
        kind = flat[:, 1 + e : 2 + e]
        for p in range(2):
            pick = jnp.where(2 * kind + p == type_lane, 1.0, 0.0).astype(BF16)
            ops[e, p] = dot(pick, operators).reshape(LINE, 8, S)
        good = jnp.logical_and(slots[:, :, 3 + e : 4 + e] == lane % B, lane // B == slot_y)
        hot.append(jnp.where(good, 1.0, 0.0)[:, None])
    spread = jnp.concatenate(hot, axis=1).reshape(2 * 128, 128)
    hm[...] = jnp.transpose(spread)[: NY * B].astype(BF16)

    def piece(z, core, q):
        return xg.at[z * NC + core, pl.ds(q * QROWS, QROWS)]

    def to_right(z, q):
        return remote(piece(z, c, q), piece(z, c, q), right_ss.at[z, q], right_rs.at[z, q], zr_dev)

    def to_left(z, q):
        return remote(piece(z, c, q), piece(z, c, q), left_ss.at[z, q], left_rs.at[z, q], zl_dev)

    def to_sib(z, q):
        return remote(piece(z, c, q), piece(z, c, q), sib_ss.at[z, q], sib_rs.at[z, q], sib_dev)

    def from_sib(z, q):
        there = piece(z, 1 - c, q)
        return remote(there, there, sib_ss.at[z, q], sib_rs.at[z, q], sib_dev)

    def translate(slot, q):
        index = jnp.broadcast_to(jnp.maximum(tr[slot][:, 0:1], 0), (8, S))
        op = [[ops[e, p, slot] for p in range(2)] for e in range(PER)]
        at = pl.multiple_of(slot * 16, 16)
        for k in range(RQ):
            r = q * RQ + k
            both = xg[slot, pl.ds(r * 16, 16), :].astype(F32)
            re = jnp.take_along_axis(both[:8], index, axis=0)
            im = jnp.take_along_axis(both[8:], index, axis=0)
            real = [op[e][0] * re - op[e][1] * im for e in range(PER)]
            imag = [op[e][0] * im + op[e][1] * re for e in range(PER)]
            pb[r, 0, pl.ds(at, 16), :] = jnp.concatenate(real, axis=0).astype(BF16)
            pb[r, 1, pl.ds(at, 16), :] = jnp.concatenate(imag, axis=0).astype(BF16)

    def own_piece(q):
        for k in range(1, 4):
            second_copy(k, q).wait_recv()
        level_step(xb[1, q], xm[0, q], lambda p, k: itp[p, 1, k], xb.at[2, q])
        level_step(xm[1, q], xm[2, q], lambda p, k: wp[p, k], yb.at[1, q])
        level_step(xb[2, q], yb[1, q], lambda p, k: itp[p, 2, k], xg.at[g, pl.ds(q * QROWS, QROWS)])

        @pl.when(zl < NZ - 1)
        def _():
            to_right(zl, q).start()

        @pl.when(zl > 0)
        def _():
            to_left(zl, q).start()

        to_sib(zl, q).start()

    def sib_slot(z, q):
        from_sib(z, q).wait_recv()
        translate(z * NC + 1 - c, q)

    def step(d, q):
        lower = zl - d
        upper = zl + d

        @pl.when(lower >= 0)
        def _():
            to_right(lower, q).wait_recv()

            @pl.when(zl < NZ - 1)
            def _():
                to_right(lower, q).start()

            to_sib(lower, q).start()

        @pl.when(upper < NZ)
        def _():
            to_left(upper, q).wait_recv()

            @pl.when(zl > 0)
            def _():
                to_left(upper, q).start()

            to_sib(upper, q).start()

        @pl.when(lower + 1 >= 0)
        def _():
            translate((lower + 1) * NC + c, q)
            sib_slot(lower + 1, q)

        @pl.when(jnp.logical_and(d > 1, upper - 1 < NZ))
        def _():
            translate((upper - 1) * NC + c, q)
            sib_slot(upper - 1, q)

    for p in range(2):
        weight_copy(p).wait_recv()
    for q in range(Q):
        own_piece(q)

    def distance(d, carry):
        for q in range(Q):
            step(d, q)
            near_one(4 * (d - 1) + q)
        return carry

    lax.fori_loop(1, NZ - 1, distance, 0)
    for n in range(NEAR - 8, NEAR):
        near_one(n)

    def y_copy(k, h):
        to = (y + k) % NY
        part = pl.ds(h * HROWS, HROWS)
        return remote(
            sb.at[to, part], yr.at[y, part], y_ss.at[k, h], y_rs.at[k, h], ((box + k * LINE) % (NY * LINE), samp)
        )

    def in_rows(total):
        cuts = [
            total[2 * r : 2 * r + 2, q * 2 * M : (q + 1) * 2 * M] for r in range(2) for q in range(B // 2)
        ]
        return jnp.concatenate(cuts, axis=0)

    def fin_copy(s):
        return remote(fb.at[s], fr.at[samp], fin_ss.at[s], fin_rs.at[samp], (box, s))

    weights = hm[...]

    def finish(h):
        for k in range(RH):
            r = h * RH + k
            real = dot(weights, pb[r, 0])
            imag = dot(weights, pb[r, 1])
            for q in range(NY):
                both = jnp.concatenate([real[q * B : (q + 1) * B], imag[q * B : (q + 1) * B]], axis=0)
                sf[q, pl.ds(r * 16, 16), :] = both
                sb[q, pl.ds(r * 16, 16), :] = both.astype(BF16)
        for k in range(1, NY):
            y_copy(k, h).start()

    for q in range(Q):
        step(NZ - 1, q)
        step(NZ, q)
        finish(q)

    def near_add(n, carry):
        target = nidx_s[0, n] - first - B
        value = near_y[n]
        return tuple(
            total + value * jnp.where(target == d, 1.0, 0.0) for d, total in enumerate(carry)
        )

    sums = lax.fori_loop(
        0, NEAR, near_add, tuple(jnp.zeros((2 * R, M), F32) for _ in range(B)), unroll=2
    )
    for q in range(B // 2):
        near2d[q] = jnp.concatenate([sums[2 * q], sums[2 * q + 1]], axis=1)

    for h in range(H):
        part = pl.ds(h * HROWS, HROWS)
        incoming = sf[y, part, :]
        for k in range(1, NY):
            y_copy(NY - k, h).wait_recv()
            incoming = incoming + yr[(y + k) % NY, part, :].astype(F32)
        rounded = incoming.astype(BF16)
        a = dot_nt(rounded, rad[0].reshape(B * M, S)).reshape(RH, 2, B, B * M)
        b = dot_nt(rounded, rad[1].reshape(B * M, S)).reshape(RH, 2, B, B * M)
        far = [a[:, 0] + b[:, 1], a[:, 1] - b[:, 0]]
        for p in range(2):
            picked = jnp.sum(jnp.where(own_box[None], far[p], 0.0), axis=1) * FAR_SCALE
            near = [near2d[q, pl.ds(h * 2 * RH + p, RH, stride=2), :] for q in range(B // 2)]
            total = picked + jnp.concatenate(near, axis=1)
            for k in range(RH):
                r = h * RH + k
                fs[r // 2, pl.ds(r % 2 * 2 + p, 1), :] = total[k : k + 1]
        for s in range(h * NS // H, (h + 1) * NS // H):
            fb[s] = in_rows(fs[s]).astype(BF16)

            @pl.when(s != samp)
            def _():
                fin_copy(s).start()

    for h in range(H):
        first_copy(h).wait_send()
        for k in range(1, 4):
            second_copy(k, h).wait_send()
    for p in range(2):
        weight_copy(p).wait_send()

    @pl.when(has_next)
    def _():
        to_next.wait_send()

    @pl.when(has_prev)
    def _():
        to_prev.wait_send()

    for k in range(1, LINE):
        table_copy(k).wait_send()
    for k in range(1, NY):
        for h in range(H):
            y_copy(k, h).wait_send()

    def drain(z, carry):
        for q in range(Q):

            @pl.when(jnp.logical_and(z <= zl, zl < NZ - 1))
            def _():
                to_right(z, q).wait_send()

            @pl.when(jnp.logical_and(z >= zl, zl > 0))
            def _():
                to_left(z, q).wait_send()

            to_sib(z, q).wait_send()
        return carry

    lax.fori_loop(0, NZ, drain, 0)
    own = fs[samp]
    others = jnp.zeros((2 * B, 2 * M), F32)
    for k in range(1, NS):
        s = (samp + k) % NS
        there = remote(fb.at[s], fr.at[s], fin_ss.at[s], fin_rs.at[s], (box, s))
        there.wait_recv()
        others = others + fr[s].astype(F32)
    out_ref[0] = in_rows(own)
    out_ref[1] = others

    for k in range(1, NS):
        fin_copy((samp + k) % NS).wait_send()


def local(
    currents, radiation, interp, translation, inter_owner, inter_local, inter_type, near_blocks, near_index
):
    hbm = pl.BlockSpec(memory_space=pl.ANY)
    smem = pltpu.SMEM
    dma = pltpu.SemaphoreType.DMA
    vmem = pltpu.VMEM
    rows = pl.pallas_call(
        kernel,
        out_shape=jax.ShapeDtypeStruct((2, 2 * B, 2 * M), F32),
        in_specs=[hbm] * 9,
        out_specs=pl.BlockSpec(memory_space=pltpu.VMEM),
        scratch_shapes=[
            smem((OWN, B), jnp.int32),
            smem((OWN * PER, B), jnp.int32),
            smem((OWN * PER, B), jnp.int32),
            smem((2, NEAR), jnp.int32),
            vmem((R, 2, B * M), BF16),
            vmem((2, R, 2, B * M), BF16),
            vmem((2, B, M, S), BF16),
            vmem((2, 3, 2, S, S), BF16),
            vmem((TYPES, 2, S), BF16),
            vmem((TROWS, S), F32),
            vmem((2, NEAR, M, M), BF16),
            vmem((3, 2 * R, B * M), F32),
            vmem((ROWS, B * M), BF16),
            vmem((2, 3 * B, 2 * R, M), BF16),
            vmem((NEAR, 2 * R, M), F32),
            vmem((B // 2, 2 * R, 2 * M), F32),
            vmem((3, H, HROWS, S), BF16),
            vmem((2, H, HROWS, S), BF16),
            vmem((3, H, HROWS, S), BF16),
            vmem((2, 2, S, S), BF16),
            vmem((LINE, ROWS, S), BF16),
            vmem((LINE, 8, 128), jnp.int32),
            vmem((LINE, 8, 128), jnp.int32),
            vmem((PER, 2, LINE, 8, S), F32),
            vmem((R, 2, 2 * 128, S), BF16),
            vmem((NY * B, 2 * 128), BF16),
            vmem((NY, ROWS, S), BF16),
            vmem((NY, ROWS, S), F32),
            vmem((NY, ROWS, S), BF16),
            vmem((NS, 4, B * M), F32),
            vmem((NS, 2 * B, 2 * M), BF16),
            vmem((NS, 2 * B, 2 * M), BF16),
            dma((9,)),
            dma((2,)),
            dma((2,)),
            dma((4, H)),
            dma((4, H)),
            dma((2,)),
            dma((2,)),
            dma((LINE,)),
            dma((LINE,)),
            dma((NZ, Q)),
            dma((NZ, Q)),
            dma((NZ, Q)),
            dma((NZ, Q)),
            dma((NZ, Q)),
            dma((NZ, Q)),
            dma((NY, H)),
            dma((NY, H)),
            dma((NS,)),
            dma((NS,)),
        ],
        compiler_params=pltpu.CompilerParams(
            collective_id=0, has_side_effects=True, vmem_limit_bytes=56 * 2**20
        ),
    )(
        currents,
        radiation,
        interp,
        jnp.transpose(translation, (1, 0, 2)),
        near_blocks,
        inter_owner.T,
        jnp.transpose(inter_local, (1, 2, 0)).reshape(OWN * PER, B),
        jnp.transpose(inter_type, (1, 2, 0)).reshape(OWN * PER, B),
        near_index.T,
    )
    return (rows[0] + rows[1]).reshape(2, B // 2, 2, 2 * M).transpose(0, 2, 1, 3).reshape(2, 2, B * M)


def solution(mesh):
    in_specs = (
        P(None, None, "box"),
        P(None, "box", None, "samp"),
        P(None, None, None, "samp", None),
        P(None, None, "samp"),
        P("box", None),
        P("box", None, None),
        P("box", None, None),
        P(None, ("box", "samp"), None, None),
        P(("box", "samp"), None),
    )
    return jax.shard_map(local, mesh=mesh, in_specs=in_specs, out_specs=P("samp", None, "box"), check_vma=False)
```
